32 devices in a mesh: ctx: 4 (over y, x), exp: 8 (over z, core).
Axes of the slice: x: 2, y: 2, z: 4, core: 2. Of those that a mesh axis runs over, the one named last changes fastest.
Arguments:
- query: bfloat16 [8, 512, 2048], P('exp', 'ctx'), may hold values from -8 to 8
- key_value: bfloat16 [8, 512, 256], P('exp', 'ctx'), may hold values from -8 to 8
- prior_out: bfloat16 [8, 512, 2048], P('exp', 'ctx'), may hold values from -6 to 6
- prior_lse: float32 [8, 512, 32], P('exp', 'ctx'), may hold values from 5 to 9
- norm_gain: float32 [2048], replicated, may hold values from 0.25 to 1.75
- w_gate: bfloat16 [8, 2048, 768], P('exp'), may hold values from -0.125 to 0.125
- w_up: bfloat16 [8, 2048, 768], P('exp'), may hold values from -0.125 to 0.125
- expert_ids: int32 [8, 512, 2], P('exp', 'ctx'), may hold values from 0 to 7, all different within a row; in each aligned block of 128 rows (0 to 127, 128 to 255, ..., all dimensions but the last counted through in order) at most 48 rows name the same one
- route_weight: bfloat16 [8, 512, 2], P('exp', 'ctx'), may hold values from 0.099609375 to 1
Outputs:
- attended: bfloat16 [8, 512, 2048], P('exp', 'ctx')
- expert_hidden: bfloat16 [4, 8, 384, 768], P('ctx', 'exp')
The draws below stay inside these ranges and needn't reach their ends.
Inputs may be any that keep to these rules, and one draw needn't show every extreme that they name: `expert_ids`: each token names 2 different experts; the rows of one device name one expert at most 48 times, a bound that some block reaches.
All inputs are finite; a program needn't handle non-finite values.
Results may differ from the reference program's by a relative error of at most 0.0072.
Values may be sent and summed in bfloat16 or wider, within the bound.
A program may use at most 64 MiB of HBM per device.

```python
import math
import jax
import jax.numpy as jnp
import numpy as np
from jax import lax

HQ = 32
KVH = 2
HD = 64
FF = 768
TOK_DEV = 128
STEPS = 3
IN_FLIGHT = 2
D = 2048
SEQS = 8
SEQLEN = 512
EXPERTS = 8
CAP = 48
N_CTX = 4


def drawn_fields(key):
    base_key = jax.random.fold_in(key, 4093)
    key_query, key_pairs = jax.random.split(base_key, 2)
    query_shape = (SEQS, SEQLEN, HQ * HD)
    pair_shape = (SEQS, SEQLEN, 2 * KVH * HD)
    queries = jnp.clip(jax.random.normal(key_query, query_shape, jnp.float32), -6.0, 6.0)
    pair_field = jnp.clip(jax.random.normal(key_pairs, pair_shape, jnp.float32), -6.0, 6.0)
    return (queries, pair_field)


def draw_query(key, part):
    return drawn_fields(key)[0].astype(jnp.bfloat16)


def draw_key_value(key, part):
    return drawn_fields(key)[1].astype(jnp.bfloat16)


def block_scale(rng, dims, pieces, low, largest):
    def one(dim, parts):
        heights = jax.random.uniform(jax.random.fold_in(jax.random.fold_in(rng, 6), dim), (parts,), jnp.float32, low / len(pieces), largest / len(pieces))
        return jnp.repeat(jnp.exp(heights), dims[dim] // parts).reshape((-1,) + (1,) * (len(dims) - dim - 1))

    factor_of = one(*pieces[0])
    for cut in pieces[1:]:
        factor_of = factor_of * one(*cut)
    return factor_of


def deal_out(key, own, number, rows, amount, top, bound, skew):
    ranking = jax.random.permutation(key, amount)
    packed, common = load_shares(amount, rows * top, bound, skew, True), load_shares(amount, rows * top, bound, skew, False)
    places = jnp.arange(amount)

    def named(lengths, offset_by):
        used = int((lengths > 0).sum())
        fixed = max(1, used // 4)
        passed = fixed + (places - fixed + offset_by * (used - fixed)) % max(1, amount - fixed)
        return jnp.zeros((amount,), jnp.int32).at[ranking[jnp.where(places < fixed, places, passed)]].set(jnp.asarray(lengths, jnp.int32))

    lengths = jnp.where(number % 4 == 0, named(packed, number // 4), named(common, number - number // 4 - 1))
    mixed = jax.random.permutation(jax.random.fold_in(own, 3), amount)
    giver, receiver = mixed[0:amount // 2 * 2:2], mixed[1:amount // 2 * 2:2]
    margin = jnp.minimum(lengths[giver] - 1, bound - lengths[receiver]) // 2
    margin = jnp.where((giver == ranking[0]) | (receiver == ranking[0]) | (lengths[receiver] == 0), 0, jnp.maximum(margin, 0))
    passed = jax.random.randint(jax.random.fold_in(own, 4), (amount // 2,), 0, 1 << 20) % (margin + 1)
    lengths = lengths.at[giver].add(-passed).at[receiver].add(passed)
    items = jnp.searchsorted(jnp.cumsum(lengths), jnp.arange(rows * top), side="right").astype(jnp.int32)
    table = items.reshape(top, rows).T
    table = table[jax.random.permutation(jax.random.fold_in(own, 1), rows)]
    offset_by = jax.random.randint(jax.random.fold_in(own, 2), (rows, 1), 0, top)
    return jnp.take_along_axis(table, (jnp.arange(top)[None, :] + offset_by) % top, axis=1)


def load_shares(amount, total, reach, slope, full):
    loads = [(1 << 20) // math.isqrt(grade ** slope) + 1 for grade in range(1, amount + 1)]
    largest = reach if full else min(reach, max(-(-total // amount), total * loads[0] // sum(loads)))
    least = 1 if total - largest >= amount - 1 else 0
    given, surplus = [largest] + [least] * (amount - 1), total - largest - least * (amount - 1)
    while surplus > 0:
        free = [i for i in range(1, amount) if given[i] < largest] or [i for i in range(1, amount) if given[i] < reach]
        pool, left = sum([loads[i] for i in free]), surplus
        for i in free:
            more = min(reach - given[i], max(1, left * loads[i] // pool), surplus)
            given[i] = given[i] + more
            surplus = surplus - more
    return np.array(given)


def centred(own_key, extent, width, most, pieces=(), held_as=jnp.bfloat16):
    gain = block_scale(own_key, extent, pieces, -0.22, 0.18) if pieces else 1.0
    values = jax.random.normal(own_key, extent, jnp.float32) * width * gain
    return jnp.minimum(jnp.maximum(values, -most), most).astype(held_as)


def setup_inputs(seed: int = 0) -> dict:
    seeds = jax.random.split(jax.random.key(seed), 10)
    query = draw_query(jax.random.fold_in(seeds[9], 71), 0)
    key_value = draw_key_value(jax.random.fold_in(seeds[9], 71), 0)
    prior_out = centred(seeds[2], (SEQS, SEQLEN, D), 1.0, 6.0, ((0, 8), (1, 4)))
    prior_lse = jnp.clip(5.0 + 4.0 * jax.random.uniform(seeds[3], (SEQS, SEQLEN, HQ), jnp.float32) ** block_scale(seeds[3], (SEQS, SEQLEN, HQ), ((0, 8), (1, 4)), -0.2, 0.2), 5.0, 9.0)
    norm_gain = jnp.clip(1.0 + 0.15 * jax.random.normal(seeds[4], (D,), jnp.float32), 0.25, 1.75)
    w_gate = centred(seeds[5], (EXPERTS, D, FF), D ** -0.5, 0.125, ((0, 8),))
    w_up = centred(seeds[6], (EXPERTS, D, FF), D ** -0.5, 0.125, ((0, 8),))
    expert_ids_keys = jax.random.split(jax.random.fold_in(seeds[7], 1), SEQS * SEQLEN // TOK_DEV)
    expert_ids_turns = jax.random.permutation(jax.random.fold_in(seeds[7], 3), SEQS * SEQLEN // TOK_DEV)
    expert_ids = jax.vmap(lambda own, number: deal_out(jax.random.fold_in(seeds[7], 2), own, number, TOK_DEV, EXPERTS, IN_FLIGHT, CAP, 2))(expert_ids_keys, expert_ids_turns).reshape((SEQS, SEQLEN, IN_FLIGHT))
    route_weight = jnp.clip(jnp.exp(math.log(1.0) - 2.306499 * jax.random.uniform(seeds[8], (SEQS, SEQLEN, IN_FLIGHT), jnp.float32) ** block_scale(seeds[8], (SEQS, SEQLEN, IN_FLIGHT), ((0, 8), (1, 4)), -0.2, 0.2)), 0.099609375, 1.0).astype(jnp.bfloat16)
    return dict(query=query, key_value=key_value, prior_out=prior_out, prior_lse=prior_lse, norm_gain=norm_gain, w_gate=w_gate, w_up=w_up, expert_ids=expert_ids, route_weight=route_weight)


def folded_positions(block_index, row_count, block_total):
    offset = jnp.arange(row_count, dtype=jnp.int32)
    half_rows = row_count // 2
    return jnp.where(offset < half_rows, block_index * half_rows + offset, (2 * block_total - 1 - block_index) * half_rows + offset - half_rows)

def attend_block(queries, window, window_pos, query_pos, prior_rows, prior_logs):
    row_count = queries.shape[0]
    group_size = HQ // KVH
    grouped = queries.astype(jnp.float32).reshape(row_count, KVH, group_size, HD)
    key_rows = window[:, :KVH * HD].astype(jnp.float32).reshape(-1, KVH, HD)
    value_rows = window[:, KVH * HD:].astype(jnp.float32).reshape(-1, KVH, HD)
    scores = jnp.einsum('tgjd,sgd->tgjs', grouped, key_rows) * HD ** (-0.5)
    allowed = (window_pos[None, :] <= query_pos[:, None])[:, None, None, :]
    scores = jnp.where(allowed, scores, -1e+30)
    logs = prior_logs.reshape(row_count, KVH, group_size)
    row_max = jnp.maximum(lax.optimization_barrier(jnp.max(scores, axis=-1)), logs)
    powers = jnp.exp(scores - row_max[..., None])
    carried = jnp.exp(logs - row_max)
    denominator = carried + lax.optimization_barrier(jnp.sum(powers, axis=-1))
    powers_low = lax.optimization_barrier(powers.astype(jnp.bfloat16)).astype(jnp.float32)
    mixed = jnp.einsum('tgjs,sgd->tgjd', powers_low, value_rows)
    earlier = prior_rows.astype(jnp.float32).reshape(row_count, KVH, group_size, HD)
    result = (carried[..., None] * earlier + mixed) / denominator[..., None]
    return result.reshape(row_count, HQ * HD).astype(jnp.bfloat16)

def normalize(row_block, gain_row):
    values = row_block.astype(jnp.float32)
    inverse = lax.rsqrt(lax.optimization_barrier(jnp.mean(values * values, axis=-1, keepdims=True)) + 1e-06)
    return (values * inverse * gain_row).astype(jnp.bfloat16)

def slot_sources(ids_flat, expert_total, capacity):
    assign_total = ids_flat.shape[0]
    onehot = (ids_flat[:, None] == jnp.arange(expert_total, dtype=jnp.int32)[None, :]).astype(jnp.int32)
    before = jnp.cumsum(onehot, axis=0) - onehot
    rank = lax.optimization_barrier(jnp.sum(before * onehot, axis=1))
    slot_of = ids_flat * capacity + rank
    match = slot_of[None, :] == jnp.arange(expert_total * capacity, dtype=jnp.int32)[:, None]
    numbered = jnp.arange(assign_total, dtype=jnp.int32)[None, :] + 1
    return lax.optimization_barrier(jnp.sum(jnp.where(match, numbered, 0), axis=1)) - 1

def reference(query, key_value, prior_out, prior_lse, norm_gain, w_gate, w_up, expert_ids, route_weight):
    seq_total = query.shape[0]
    query_blocks = query.reshape(seq_total, N_CTX, TOK_DEV, HQ * HD)
    pair_blocks = key_value.reshape(seq_total, N_CTX, TOK_DEV, 2 * KVH * HD)
    prior_blocks = prior_out.reshape(seq_total, N_CTX, TOK_DEV, HQ * HD)
    log_blocks = prior_lse.reshape(seq_total, N_CTX, TOK_DEV, HQ)
    step_list = jnp.arange(STEPS, dtype=jnp.int32)

    def block_positions(block_index):
        return folded_positions(block_index, TOK_DEV, N_CTX)

    def one_sequence(sequence):
        pairs_here = pair_blocks[sequence]

        def one_block(block_index, queries, prior_rows, prior_logs):
            sources = (block_index - step_list) % N_CTX
            window = pairs_here[sources].reshape(STEPS * TOK_DEV, 2 * KVH * HD)
            window_pos = jax.vmap(block_positions)(sources).reshape(-1)
            query_pos = block_positions(block_index)
            return attend_block(queries, window, window_pos, query_pos, prior_rows, prior_logs)
        return jax.vmap(one_block)(jnp.arange(N_CTX, dtype=jnp.int32), query_blocks[sequence], prior_blocks[sequence], log_blocks[sequence])
    attended = lax.map(one_sequence, jnp.arange(seq_total, dtype=jnp.int32))
    normed = normalize(attended, norm_gain)
    ids_dev = expert_ids.reshape(seq_total, N_CTX, TOK_DEV * IN_FLIGHT)
    weight_dev = route_weight.reshape(seq_total, N_CTX, TOK_DEV * IN_FLIGHT)

    def table_row(ids_flat):
        return slot_sources(ids_flat, EXPERTS, CAP)
    slot_table = jax.vmap(jax.vmap(table_row))(ids_dev)
    seq_index = jnp.arange(seq_total, dtype=jnp.int32)[None, :, None]
    ctx_index = jnp.arange(N_CTX, dtype=jnp.int32)[:, None, None]

    def expert_block(expert):
        chosen = lax.dynamic_slice_in_dim(slot_table, expert * CAP, CAP, 2)
        chosen = jnp.transpose(chosen, (1, 0, 2))
        filled = chosen >= 0
        clamped = jnp.maximum(chosen, 0)
        row_block = normed[seq_index, ctx_index, clamped // IN_FLIGHT]
        row_block = jnp.where(filled[..., None], row_block, jnp.zeros((), jnp.bfloat16))
        weights = jnp.where(filled, weight_dev[seq_index, ctx_index, clamped], jnp.zeros((), jnp.bfloat16))
        flat_rows = row_block.reshape(-1, HQ * HD)
        gate_out = jnp.dot(flat_rows, w_gate[expert], preferred_element_type=jnp.float32)
        up_out = jnp.dot(flat_rows, w_up[expert], preferred_element_type=jnp.float32)
        hidden = jax.nn.silu(gate_out) * up_out * weights.astype(jnp.float32).reshape(-1)[:, None]
        return hidden.astype(jnp.bfloat16).reshape(N_CTX, seq_total * CAP, FF)
    expert_hidden = lax.map(expert_block, jnp.arange(EXPERTS, dtype=jnp.int32))
    expert_hidden = jnp.transpose(expert_hidden, (1, 0, 2, 3))
    return (attended.reshape(seq_total, N_CTX * TOK_DEV, HQ * HD), expert_hidden)
```

```python
import functools

import jax
import jax.numpy as jnp
from jax import lax
from jax.experimental import pallas as pl
from jax.experimental.pallas import tpu as pltpu
from jax.sharding import PartitionSpec as P

HQ = 32
KVH = 2
HD = 64
FF = 768
STEPS = 3
IN_FLIGHT = 2

MESH = pl.DeviceIdType.MESH
WIDE = 256
QUAD = WIDE // HD
F32 = jnp.float32
BF16 = jnp.bfloat16


def dot(a, b, contract=((1,), (0,))):
    return lax.dot_general(a, b, (contract, ((), ())), preferred_element_type=F32)


def iota(shape, dim):
    return lax.broadcasted_iota(jnp.int32, shape, dim)


def positions(block, offset, rows, total):
    half = rows // 2
    return jnp.where(
        offset < half, block * half + offset, (2 * total - 1 - block) * half + offset - half
    )


def spread(columns, rows):
    lane_head = iota((rows, WIDE), 1) // HD
    out = jnp.broadcast_to(columns[QUAD - 1], (rows, WIDE))
    for i in range(QUAD - 2, -1, -1):
        out = jnp.where(lane_head == i, columns[i], out)
    return out


def kernel(
    ctx_total, exp_total, cap,
    query, key_value, prior_out, prior_lse, gain, w_gate, w_up, ids, weights,
    attended_out, hidden_out,
    q, prior, wg, wu, window, keys, values, attended, pick, send, recv,
    meta_send, meta_recv, normed, hidden,
    local_sem, kv_send, kv_recv, row_send, row_recv, meta_send_sem, meta_recv_sem,
):
    rows = q.shape[0]
    width = q.shape[1]
    chunks = width // WIDE
    span = STEPS * rows
    me = lax.axis_index("exp")
    ctx = lax.axis_index("ctx")

    loads = [
        pltpu.make_async_copy(a, b, local_sem.at[i])
        for i, (a, b) in enumerate(((query, q), (prior_out, prior), (w_gate, wg), (w_up, wu)))
    ]
    for load in loads:
        load.start()

    steps = sorted({d % ctx_total for j in range(1, STEPS) for d in (j, -j)})
    barrier = pltpu.get_barrier_semaphore()
    for d in steps:
        pl.semaphore_signal(
            barrier, inc=1, device_id={"ctx": lax.rem(ctx + d, ctx_total)}, device_id_type=MESH
        )

    def greet(d, _):
        pl.semaphore_signal(
            barrier, inc=1, device_id={"exp": lax.rem(me + d, exp_total)}, device_id_type=MESH
        )
        return 0

    lax.fori_loop(1, exp_total, greet, 0)
    pl.semaphore_wait(barrier, exp_total - 1 + len(steps))

    passes = [
        pltpu.make_async_remote_copy(
            src_ref=key_value, dst_ref=window.at[j - 1],
            send_sem=kv_send.at[j - 1], recv_sem=kv_recv.at[j - 1],
            device_id={"ctx": lax.rem(ctx + j, ctx_total)}, device_id_type=MESH,
        )
        for j in range(1, STEPS)
    ]
    for one in passes:
        one.start()

    eye = (iota((rows, rows), 0) == iota((rows, rows), 1)).astype(BF16)
    id_rows = dot(ids[...].astype(F32).astype(BF16), eye, ((0,), (0,))).astype(jnp.int32)
    weight_rows = dot(weights[...], eye, ((0,), (0,)))
    experts = iota((exp_total, rows), 0)
    named = jnp.zeros((exp_total, rows), F32)
    named_weight = jnp.zeros((exp_total, rows), F32)
    for j in range(IN_FLIGHT):
        hit = (experts == id_rows[j : j + 1, :]).astype(F32)
        named = named + hit
        named_weight = named_weight + hit * weight_rows[j : j + 1, :]
    earlier = (iota((rows, rows), 0) < iota((rows, rows), 1)).astype(BF16)
    rank = dot(named.astype(BF16), earlier).astype(jnp.int32)
    rank = jnp.where(named > 0.5, rank, -1)
    slot = iota((cap, rows), 0)
    for e in range(exp_total):
        chosen = (slot == rank[e : e + 1, :]).astype(BF16)
        pick[e * cap : (e + 1) * cap, :] = chosen
        column = jnp.sum(
            chosen.astype(F32) * named_weight[e : e + 1, :], axis=1, keepdims=True
        )
        diagonal = (iota((cap, rows), 0) == iota((cap, rows), 1)).astype(F32)
        line = jnp.sum(diagonal * column, axis=0, keepdims=True)
        meta_send[e] = jnp.broadcast_to(line, (8, rows))

    def meta_copy(to, at):
        return pltpu.make_async_remote_copy(
            src_ref=meta_send.at[to], dst_ref=meta_recv.at[at],
            send_sem=meta_send_sem.at[to], recv_sem=meta_recv_sem.at[at],
            device_id={"exp": to}, device_id_type=MESH,
        )

    def start_meta(d, _):
        meta_copy(lax.rem(me + d, exp_total), me).start()
        return 0

    lax.fori_loop(1, exp_total, start_meta, 0)
    meta_recv[me] = meta_send[me]

    own = iota((rows, 1), 0)
    query_pos = positions(ctx, own, rows, ctx_total)
    bias = []
    for j in range(STEPS):
        source = lax.rem(ctx - j + ctx_total, ctx_total)
        key_pos = positions(source, iota((1, rows), 1), rows, ctx_total)
        bias.append(jnp.where(key_pos <= query_pos, 0.0, -1e30))
    bias = jnp.concatenate(bias, axis=1)

    for one in passes:
        one.wait_recv()
    for j in range(STEPS):
        block = key_value[...] if j == 0 else window[j - 1]
        block_keys = block[:, : KVH * HD] * jnp.asarray(HD ** (-0.5), BF16)
        block_values = block[:, KVH * HD :]
        for g in range(KVH):
            for i in range(QUAD):
                row = iota((KVH * HD, WIDE), 0)
                lane = iota((KVH * HD, WIDE), 1)
                place = (
                    (row - g * HD == lane - i * HD) & (lane // HD == i)
                ).astype(BF16)
                at = i * span + j * rows
                keys[g, at : at + rows, :] = dot(block_keys, place).astype(BF16)
                values[g, at : at + rows, :] = dot(block_values, place).astype(BF16)

    loads[0].wait()
    loads[1].wait()

    def row_copy(c, to, at):
        return pltpu.make_async_remote_copy(
            src_ref=send.at[c, pl.ds(pl.multiple_of(to * cap, cap), cap)],
            dst_ref=recv.at[c, pl.ds(pl.multiple_of(at * cap, cap), cap)],
            send_sem=row_send.at[c, to], recv_sem=row_recv.at[c, at],
            device_id={"exp": to}, device_id_type=MESH,
        )

    mine = pl.ds(pl.multiple_of(me * cap, cap), cap)
    for c in range(chunks):
        lanes = slice(c * WIDE, (c + 1) * WIDE)
        g = c * QUAD // (HQ // KVH)
        scores = dot(q[:, lanes], keys[g], ((1,), (1,)))
        powers, carried, total = [], [], []
        for i in range(QUAD):
            part = scores[:, i * span : (i + 1) * span] + bias
            head = c * QUAD + i
            logs = prior_lse[:, head : head + 1]
            row_max = jnp.maximum(jnp.max(part, axis=1, keepdims=True), logs)
            power = jnp.exp(part - row_max)
            share = jnp.exp(logs - row_max)
            carried.append(share)
            total.append(share + jnp.sum(power, axis=1, keepdims=True))
            powers.append(power.astype(BF16))
        mixed = dot(jnp.concatenate(powers, axis=1), values[g])
        result = (
            spread(carried, rows) * prior[:, lanes].astype(F32) + mixed
        ) / spread(total, rows)
        result = result.astype(BF16)
        attended[:, lanes] = result
        send[c] = dot(pick[...], result).astype(BF16)

        def start_rows(d, _, c=c):
            row_copy(c, lax.rem(me + d, exp_total), me).start()
            return 0

        lax.fori_loop(1, exp_total, start_rows, 0)
        recv[c, mine, :] = send[c, mine, :]

    store = pltpu.make_async_copy(attended, attended_out, local_sem.at[0])
    store.start()

    squares = jnp.zeros((exp_total * cap, 1), F32)
    for c in range(chunks):

        def land(d, _, c=c):
            row_copy(c, me, lax.rem(me + d, exp_total)).wait_recv()
            return 0

        lax.fori_loop(1, exp_total, land, 0)
        block = recv[c].astype(F32)
        squares = squares + jnp.sum(block * block, axis=1, keepdims=True)
    inverse = lax.rsqrt(squares / width + 1e-6)
    for c in range(chunks):
        lanes = slice(c * WIDE, (c + 1) * WIDE)
        normed[:, lanes] = (recv[c].astype(F32) * inverse * gain[:, lanes]).astype(BF16)

    def land_meta(d, _):
        meta_copy(me, lax.rem(me + d, exp_total)).wait_recv()
        return 0

    lax.fori_loop(1, exp_total, land_meta, 0)
    diagonal = (iota((cap, rows), 0) == iota((cap, rows), 1)).astype(F32)
    slot_weight = jnp.concatenate(
        [
            jnp.sum(diagonal * meta_recv[s][:1, :], axis=1, keepdims=True)
            for s in range(exp_total)
        ],
        axis=0,
    )
    loads[2].wait()
    loads[3].wait()
    stores = []
    for n in range(wg.shape[1] // WIDE):
        lanes = slice(n * WIDE, (n + 1) * WIDE)
        gate = dot(normed[...], wg[:, lanes])
        up = dot(normed[...], wu[:, lanes])
        hidden[:, lanes] = (gate / (1.0 + jnp.exp(-gate)) * up * slot_weight).astype(BF16)
        out = pltpu.make_async_copy(
            hidden.at[:, lanes], hidden_out.at[:, lanes], local_sem.at[1 + n]
        )
        out.start()
        stores.append(out)

    for one in passes:
        one.wait_send()

    def sent(d, _):
        to = lax.rem(me + d, exp_total)
        meta_copy(to, me).wait_send()
        for c in range(chunks):
            row_copy(c, to, me).wait_send()
        return 0

    lax.fori_loop(1, exp_total, sent, 0)
    store.wait()
    for out in stores:
        out.wait()


def per_device(
    query, key_value, prior_out, prior_lse, norm_gain, w_gate, w_up, expert_ids, route_weight
):
    ctx_total = lax.axis_size("ctx")
    exp_total = lax.axis_size("exp")
    rows, width = query.shape[1:]
    hidden_width = w_gate.shape[2]
    capacity = max(2, IN_FLIGHT * rows * 3 // (2 * exp_total))
    cap = -(-capacity // 16) * 16
    chunks = width // WIDE
    pair_width = key_value.shape[2]
    any_space = pl.BlockSpec(memory_space=pl.ANY)
    vmem = pl.BlockSpec(memory_space=pltpu.VMEM)
    dma = pltpu.SemaphoreType.DMA
    slots = exp_total * cap
    attended, hidden = pl.pallas_call(
        functools.partial(kernel, ctx_total, exp_total, cap),
        out_shape=(
            jax.ShapeDtypeStruct((rows, width), BF16),
            jax.ShapeDtypeStruct((slots, hidden_width), BF16),
        ),
        in_specs=[any_space, vmem, any_space, vmem, vmem, any_space, any_space, vmem, vmem],
        out_specs=(any_space, any_space),
        scratch_shapes=[
            pltpu.VMEM((rows, width), BF16),
            pltpu.VMEM((rows, width), BF16),
            pltpu.VMEM(w_gate.shape[1:], BF16),
            pltpu.VMEM(w_up.shape[1:], BF16),
            pltpu.VMEM((STEPS - 1, rows, pair_width), BF16),
            pltpu.VMEM((KVH, QUAD * STEPS * rows, WIDE), BF16),
            pltpu.VMEM((KVH, QUAD * STEPS * rows, WIDE), BF16),
            pltpu.VMEM((rows, width), BF16),
            pltpu.VMEM((slots, rows), BF16),
            pltpu.VMEM((chunks, slots, WIDE), BF16),
            pltpu.VMEM((chunks, slots, WIDE), BF16),
            pltpu.VMEM((exp_total, 8, rows), F32),
            pltpu.VMEM((exp_total, 8, rows), F32),
            pltpu.VMEM((slots, width), BF16),
            pltpu.VMEM((slots, hidden_width), BF16),
            dma((8,)),
            dma((STEPS - 1,)),
            dma((STEPS - 1,)),
            dma((chunks, exp_total)),
            dma((chunks, exp_total)),
            dma((exp_total,)),
            dma((exp_total,)),
        ],
        compiler_params=pltpu.CompilerParams(
            collective_id=0, has_side_effects=True, vmem_limit_bytes=48 * 1024 * 1024
        ),
    )(
        query[0], key_value[0], prior_out[0], prior_lse[0], norm_gain[None], w_gate[0], w_up[0],
        expert_ids[0], route_weight[0],
    )
    hidden = hidden.reshape(exp_total, cap, hidden_width)[:, :capacity]
    return (attended[None], hidden.reshape(1, 1, exp_total * capacity, hidden_width))


def solution(mesh):
    placed = (
        P("exp", "ctx", None),
        P("exp", "ctx", None),
        P("exp", "ctx", None),
        P("exp", "ctx", None),
        P(),
        P("exp", None, None),
        P("exp", None, None),
        P("exp", "ctx", None),
        P("exp", "ctx", None),
    )
    return jax.shard_map(
        per_device,
        mesh=mesh,
        in_specs=placed,
        out_specs=(P("exp", "ctx", None), P("ctx", "exp", None, None)),
        check_vma=False,
    )
```

```python
import functools

import jax
import jax.numpy as jnp
from jax import lax
from jax.experimental import pallas as pl
from jax.experimental.pallas import tpu as pltpu
from jax.sharding import PartitionSpec as P

HQ = 32
KVH = 2
HD = 64
FF = 768
STEPS = 3
IN_FLIGHT = 2

MESH = pl.DeviceIdType.MESH
WIDE = 256
QUAD = WIDE // HD
F32 = jnp.float32
BF16 = jnp.bfloat16


def dot(a, b, contract=((1,), (0,))):
    return lax.dot_general(a, b, (contract, ((), ())), preferred_element_type=F32)


def iota(shape, dim):
    return lax.broadcasted_iota(jnp.int32, shape, dim)


def positions(block, offset, rows, total):
    half = rows // 2
    return jnp.where(
        offset < half, block * half + offset, (2 * total - 1 - block) * half + offset - half
    )


def spread(columns, rows):
    lane_head = iota((rows, WIDE), 1) // HD
    out = jnp.broadcast_to(columns[QUAD - 1], (rows, WIDE))
    for i in range(QUAD - 2, -1, -1):
        out = jnp.where(lane_head == i, columns[i], out)
    return out


def each(first, last, body):
    if last - first <= 8:
        for d in range(first, last):
            body(d)
    else:
        lax.fori_loop(first, last, lambda d, _: (body(d), 0)[1], 0)


def slot_rows(rank_ref, base, count, cap, rows):
    slot = iota((cap, rows), 0).astype(F32)
    return jnp.concatenate(
        [(slot == rank_ref[pl.ds(base + e, 1), :]).astype(BF16) for e in range(count)], axis=0
    )


def kernel(
    ctx_total, exp_total, cap,
    query, key_value, prior_out, prior_lse, gain, w_gate, w_up, ids, weights,
    attended_out, hidden_out,
    q, kv, prior, lse, scale, wg, wu, id_rows, weight_rows,
    window, keys, values, raw, pick, relay_pick, send, relay_in, relay_out, recv,
    rank_send, rank_recv, meta_send, meta_recv, normed, hidden,
    local_sem, out_sem, kv_send, kv_recv, row_send, row_recv, relay_send,
    raw_send, raw_recv, rank_sems, meta_send_sem, meta_recv_sem,
):
    rows = q.shape[0]
    width = q.shape[1]
    chunks = width // WIDE
    span = STEPS * rows
    half = exp_total // 2
    me = lax.axis_index("exp")
    ctx = lax.axis_index("ctx")
    side = me // half
    base = side * half
    local = me - base
    far = half - base
    across = lax.rem(me + half, exp_total)

    loads = [
        pltpu.make_async_copy(a, b, local_sem.at[i])
        for i, (a, b) in enumerate(
            (
                (key_value, kv), (ids, id_rows), (weights, weight_rows), (prior_lse, lse),
                (query, q), (prior_out, prior), (gain, scale), (w_gate, wg), (w_up, wu),
            )
        )
    ]
    for load in loads:
        load.start()

    steps = sorted({d % ctx_total for j in range(1, STEPS) for d in (j, -j)})
    barrier = pltpu.get_barrier_semaphore()
    for d in steps:
        pl.semaphore_signal(
            barrier, inc=1, device_id={"ctx": lax.rem(ctx + d, ctx_total)}, device_id_type=MESH
        )

    def greet(d):
        pl.semaphore_signal(
            barrier, inc=1, device_id={"exp": lax.rem(me + d, exp_total)}, device_id_type=MESH
        )

    each(1, exp_total, greet)

    loads[1].wait()
    loads[2].wait()
    experts = iota((exp_total, rows), 0)
    named = jnp.zeros((exp_total, rows), F32)
    named_weight = jnp.zeros((exp_total, rows), F32)
    for j in range(IN_FLIGHT):
        hit = (experts == id_rows[j : j + 1, :]).astype(F32)
        named = named + hit
        named_weight = named_weight + hit * weight_rows[j : j + 1, :].astype(F32)
    earlier = (iota((rows, rows), 0) < iota((rows, rows), 1)).astype(BF16)
    rank_send[...] = jnp.where(named > 0.5, dot(named.astype(BF16), earlier), -1.0)
    loads[0].wait()
    pl.semaphore_wait(barrier, exp_total - 1 + len(steps))

    passes = [
        pltpu.make_async_remote_copy(
            src_ref=kv, dst_ref=window.at[j - 1],
            send_sem=kv_send.at[j - 1], recv_sem=kv_recv.at[j - 1],
            device_id={"ctx": lax.rem(ctx + j, ctx_total)}, device_id_type=MESH,
        )
        for j in range(1, STEPS)
    ]
    for one in passes:
        one.start()
    rank_copy = pltpu.make_async_remote_copy(
        src_ref=rank_send, dst_ref=rank_recv, send_sem=rank_sems.at[0],
        recv_sem=rank_sems.at[1], device_id={"exp": across}, device_id_type=MESH,
    )
    rank_copy.start()
    pick[...] = slot_rows(rank_send, base, half, cap, rows)

    own = iota((rows, 1), 0)
    query_pos = positions(ctx, own, rows, ctx_total)
    bias = []
    for j in range(STEPS):
        source = lax.rem(ctx - j + ctx_total, ctx_total)
        key_pos = positions(source, iota((1, rows), 1), rows, ctx_total)
        bias.append(jnp.where(key_pos <= query_pos, 0.0, -1e30))
    bias = jnp.concatenate(bias, axis=1)

    place_row = iota((KVH * HD, WIDE), 0)
    place_lane = lax.rem(iota((KVH * HD, WIDE), 1), HD)
    places = [(place_row == place_lane + g * HD).astype(BF16) for g in range(KVH)]
    lane_head = iota((rows, WIDE), 1) // HD

    def lay_out(j, block):
        block_keys = block[:, : KVH * HD] * jnp.asarray(HD ** (-0.5), BF16)
        block_values = block[:, KVH * HD :]
        for g in range(KVH):
            for part, target in ((block_keys, keys), (block_values, values)):
                tiled = dot(part, places[g])
                for i in range(QUAD):
                    at = i * span + j * rows
                    target[g, at : at + rows, :] = jnp.where(lane_head == i, tiled, 0.0).astype(BF16)

    lay_out(0, kv[...])
    loads[3].wait()
    logs_all = jnp.transpose(lse[...])
    loads[4].wait()
    loads[5].wait()
    for j in range(1, STEPS):
        passes[j - 1].wait_recv()
        lay_out(j, window[j - 1])

    def slots_of(index):
        return pl.ds(pl.multiple_of(index * cap, cap), cap)

    def row_copy(c, to_local, source_ref, sems, source):
        return pltpu.make_async_remote_copy(
            src_ref=source_ref.at[c, slots_of(to_local)],
            dst_ref=recv.at[c, slots_of(source)],
            send_sem=sems.at[c, to_local], recv_sem=row_recv.at[c, source],
            device_id={"exp": base + to_local}, device_id_type=MESH,
        )

    def peer(d):
        return lax.rem(local + d, half)

    def raw_copy(c):
        return pltpu.make_async_remote_copy(
            src_ref=raw.at[c], dst_ref=relay_in.at[c], send_sem=raw_send.at[c],
            recv_sem=raw_recv.at[c], device_id={"exp": across}, device_id_type=MESH,
        )

    def out_copy(c):
        return pltpu.make_async_copy(
            raw.at[c], attended_out.at[:, c * WIDE : (c + 1) * WIDE], out_sem.at[c]
        )

    def meta_copy(to, at):
        return pltpu.make_async_remote_copy(
            src_ref=meta_send.at[to], dst_ref=meta_recv.at[at],
            send_sem=meta_send_sem.at[to], recv_sem=meta_recv_sem.at[at],
            device_id={"exp": to}, device_id_type=MESH,
        )

    def pass_on(c):
        raw_copy(c).wait_recv()
        relay_out[c] = dot(relay_pick[...], relay_in[c]).astype(BF16)
        each(1, half, lambda d: row_copy(c, peer(d), relay_out, relay_send, across).start())
        recv[c, slots_of(across), :] = relay_out[c, slots_of(local), :]

    diagonal = (iota((cap, rows), 0) == iota((cap, rows), 1)).astype(F32)

    def send_weights():
        slot = iota((cap, rows), 0).astype(F32)
        for e in range(exp_total):
            chosen = slot == rank_send[e : e + 1, :]
            column = jnp.sum(
                jnp.where(chosen, named_weight[e : e + 1, :], 0.0), axis=1, keepdims=True
            )
            line = jnp.sum(diagonal * column, axis=0, keepdims=True)
            meta_send[e] = jnp.broadcast_to(line, (8, rows))
        each(1, exp_total, lambda d: meta_copy(lax.rem(me + d, exp_total), me).start())
        meta_recv[me] = meta_send[me]

    def scores_of(c):
        g = c * QUAD // (HQ // KVH)
        return dot(q[:, c * WIDE : (c + 1) * WIDE], keys[g], ((1,), (1,)))

    lag = 2
    ahead = scores_of(0)
    for c in range(chunks):
        lanes = slice(c * WIDE, (c + 1) * WIDE)
        g = c * QUAD // (HQ // KVH)
        scores = ahead
        if c + 1 < chunks:
            ahead = scores_of(c + 1)
        powers, carried, total = [], [], []
        for i in range(QUAD):
            part = scores[:, i * span : (i + 1) * span] + bias
            head = c * QUAD + i
            logs = logs_all[:, head : head + 1]
            row_max = jnp.maximum(jnp.max(part, axis=1, keepdims=True), logs)
            power = jnp.exp(part - row_max)
            share = jnp.exp(logs - row_max)
            carried.append(share)
            total.append(share + jnp.sum(power, axis=1, keepdims=True))
            powers.append(power.astype(BF16))
        mixed = dot(jnp.concatenate(powers, axis=1), values[g])
        result = (
            spread(carried, rows) * prior[:, lanes].astype(F32) + mixed
        ) / spread(total, rows)
        result = result.astype(BF16)
        raw[c] = result
        raw_copy(c).start()
        send[c] = dot(pick[...], result).astype(BF16)
        each(1, half, lambda d: row_copy(c, peer(d), send, row_send, me).start())
        out_copy(c).start()
        recv[c, slots_of(me), :] = send[c, slots_of(local), :]
        if c == 0:
            rank_copy.wait_recv()
            relay_pick[...] = slot_rows(rank_recv, base, half, cap, rows)
        if c == 1:
            send_weights()
        if c >= lag:
            pass_on(c - lag)
    for c in range(max(0, chunks - lag), chunks):
        pass_on(c)

    loads[6].wait()
    loads[7].wait()
    loads[8].wait()
    stores = []
    for order, start in enumerate((base, far)):
        block_rows = pl.ds(pl.multiple_of(start * cap, cap), half * cap)

        def land(d, start=start, order=order):
            if order == 0:
                source = base + peer(d)
            else:
                source = far + lax.rem(local + d, half)
            meta_copy(me, source).wait_recv()
            for c in range(chunks):
                row_copy(c, local, send, row_send, source).wait_recv()

        each(1, half, land)
        if order == 1:
            meta_copy(me, across).wait_recv()
        squares = jnp.zeros((half * cap, 1), F32)
        for c in range(chunks):
            block = recv[c, block_rows, :].astype(F32)
            squares = squares + jnp.sum(block * block, axis=1, keepdims=True)
        inverse = lax.rsqrt(squares / width + 1e-6)
        for c in range(chunks):
            lanes = slice(c * WIDE, (c + 1) * WIDE)
            block = recv[c, block_rows, :].astype(F32)
            normed[:, lanes] = (block * inverse * scale[:, lanes]).astype(BF16)
        slot_weight = jnp.concatenate(
            [
                jnp.sum(diagonal * meta_recv[start + s][:1, :], axis=1, keepdims=True)
                for s in range(half)
            ],
            axis=0,
        )
        for n in range(wg.shape[1] // WIDE):
            lanes = slice(n * WIDE, (n + 1) * WIDE)
            gate = dot(normed[...], wg[:, lanes])
            up = dot(normed[...], wu[:, lanes])
            hidden[order, :, lanes] = (
                gate / (1.0 + jnp.exp(-gate)) * up * slot_weight
            ).astype(BF16)
        out = pltpu.make_async_copy(
            hidden.at[order], hidden_out.at[block_rows], local_sem.at[order]
        )
        out.start()
        stores.append(out)

    for one in passes:
        one.wait_send()
    rank_copy.wait_send()
    each(1, exp_total, lambda d: meta_copy(lax.rem(me + d, exp_total), me).wait_send())
    for c in range(chunks):
        raw_copy(c).wait_send()
        out_copy(c).wait()

    def sent(d):
        for c in range(chunks):
            row_copy(c, peer(d), send, row_send, me).wait_send()
            row_copy(c, peer(d), relay_out, relay_send, across).wait_send()

    each(1, half, sent)
    for out in stores:
        out.wait()


def per_device(
    query, key_value, prior_out, prior_lse, norm_gain, w_gate, w_up, expert_ids, route_weight
):
    ctx_total = lax.axis_size("ctx")
    exp_total = lax.axis_size("exp")
    rows, width = query.shape[1:]
    hidden_width = w_gate.shape[2]
    capacity = max(2, IN_FLIGHT * rows * 3 // (2 * exp_total))
    cap = -(-capacity // 16) * 16
    chunks = width // WIDE
    pair_width = key_value.shape[2]
    any_space = pl.BlockSpec(memory_space=pl.ANY)
    dma = pltpu.SemaphoreType.DMA
    slots = exp_total * cap
    half_slots = exp_total // 2 * cap
    attended, hidden = pl.pallas_call(
        functools.partial(kernel, ctx_total, exp_total, cap),
        out_shape=(
            jax.ShapeDtypeStruct((rows, width), BF16),
            jax.ShapeDtypeStruct((slots, hidden_width), BF16),
        ),
        in_specs=[any_space] * 9,
        out_specs=(any_space, any_space),
        scratch_shapes=[
            pltpu.VMEM((rows, width), BF16),
            pltpu.VMEM((rows, pair_width), BF16),
            pltpu.VMEM((rows, width), BF16),
            pltpu.VMEM((HQ, rows), F32),
            pltpu.VMEM((1, width), F32),
            pltpu.VMEM(w_gate.shape[1:], BF16),
            pltpu.VMEM(w_up.shape[1:], BF16),
            pltpu.VMEM((IN_FLIGHT, rows), jnp.int32),
            pltpu.VMEM((IN_FLIGHT, rows), BF16),
            pltpu.VMEM((STEPS - 1, rows, pair_width), BF16),
            pltpu.VMEM((KVH, QUAD * STEPS * rows, WIDE), BF16),
            pltpu.VMEM((KVH, QUAD * STEPS * rows, WIDE), BF16),
            pltpu.VMEM((chunks, rows, WIDE), BF16),
            pltpu.VMEM((half_slots, rows), BF16),
            pltpu.VMEM((half_slots, rows), BF16),
            pltpu.VMEM((chunks, half_slots, WIDE), BF16),
            pltpu.VMEM((chunks, rows, WIDE), BF16),
            pltpu.VMEM((chunks, half_slots, WIDE), BF16),
            pltpu.VMEM((chunks, slots, WIDE), BF16),
            pltpu.VMEM((exp_total, rows), F32),
            pltpu.VMEM((exp_total, rows), F32),
            pltpu.VMEM((exp_total, 8, rows), F32),
            pltpu.VMEM((exp_total, 8, rows), F32),
            pltpu.VMEM((half_slots, width), BF16),
            pltpu.VMEM((2, half_slots, hidden_width), BF16),
            dma((9,)),
            dma((chunks,)),
            dma((STEPS - 1,)),
            dma((STEPS - 1,)),
            dma((chunks, exp_total // 2)),
            dma((chunks, exp_total)),
            dma((chunks, exp_total // 2)),
            dma((chunks,)),
            dma((chunks,)),
            dma((2,)),
            dma((exp_total,)),
            dma((exp_total,)),
        ],
        compiler_params=pltpu.CompilerParams(
            collective_id=0, has_side_effects=True, vmem_limit_bytes=60 * 1024 * 1024
        ),
    )(
        query[0], key_value[0], prior_out[0], prior_lse[0].T, norm_gain[None], w_gate[0], w_up[0],
        expert_ids[0].T, route_weight[0].T,
    )
    hidden = hidden.reshape(exp_total, cap, hidden_width)[:, :capacity]
    return (attended[None], hidden.reshape(1, 1, exp_total * capacity, hidden_width))


def solution(mesh):
    placed = (
        P("exp", "ctx", None),
        P("exp", "ctx", None),
        P("exp", "ctx", None),
        P("exp", "ctx", None),
        P(),
        P("exp", None, None),
        P("exp", None, None),
        P("exp", "ctx", None),
        P("exp", "ctx", None),
    )
    return jax.shard_map(
        per_device,
        mesh=mesh,
        in_specs=placed,
        out_specs=(P("exp", "ctx", None), P("ctx", "exp", None, None)),
        check_vma=False,
    )
```

```python
import functools

import jax
import jax.numpy as jnp
from jax import lax
from jax.experimental import pallas as pl
from jax.experimental.pallas import tpu as pltpu
from jax.sharding import PartitionSpec as P

HQ = 32
KVH = 2
HD = 64
FF = 768
STEPS = 3
IN_FLIGHT = 2

MESH = pl.DeviceIdType.MESH
WIDE = 256
QUAD = WIDE // HD
PIECES = 4
F32 = jnp.float32
BF16 = jnp.bfloat16


def dot(a, b, contract=((1,), (0,))):
    return lax.dot_general(a, b, (contract, ((), ())), preferred_element_type=F32)


def iota(shape, dim):
    return lax.broadcasted_iota(jnp.int32, shape, dim)


def positions(block, offset, rows, total):
    half = rows // 2
    return jnp.where(
        offset < half, block * half + offset, (2 * total - 1 - block) * half + offset - half
    )


def spread(columns, rows):
    lane_head = iota((rows, WIDE), 1) // HD
    out = jnp.broadcast_to(columns[QUAD - 1], (rows, WIDE))
    for i in range(QUAD - 2, -1, -1):
        out = jnp.where(lane_head == i, columns[i], out)
    return out


def each(first, last, body):
    if last - first <= 8:
        for d in range(first, last):
            body(d)
    else:
        lax.fori_loop(first, last, lambda d, _: (body(d), 0)[1], 0)


def slot_rows(rank_ref, base, count, cap, rows):
    slot = iota((cap, rows), 0).astype(F32)
    return jnp.concatenate(
        [(slot == rank_ref[pl.ds(base + e, 1), :]).astype(BF16) for e in range(count)], axis=0
    )


def kernel(
    ctx_total, exp_total, cap,
    query, key_value, prior_out, prior_lse, gain, w_gate, w_up, ids, weights,
    attended_out, hidden_out,
    q, kv, prior, lse, scale, wg, wu, id_rows, weight_rows,
    window, keys, values, raw, pick, relay_pick, send, relay_in, relay_out, recv,
    rank_send, rank_recv, meta_send, meta_recv, squares, gates, ups, hidden,
    local_sem, out_sem, kv_send, kv_recv, row_send, row_recv, relay_send,
    raw_send, raw_recv, rank_sems, meta_send_sem, meta_recv_sem,
):
    rows = q.shape[0]
    width = q.shape[1]
    chunks = width // WIDE
    span = STEPS * rows
    half = exp_total // 2
    me = lax.axis_index("exp")
    ctx = lax.axis_index("ctx")
    side = me // half
    base = side * half
    local = me - base
    far = half - base
    across = lax.rem(me + half, exp_total)

    loads = [
        pltpu.make_async_copy(a, b, local_sem.at[i])
        for i, (a, b) in enumerate(
            (
                (key_value, kv), (ids, id_rows), (weights, weight_rows), (prior_lse, lse),
                (query, q), (prior_out, prior), (gain, scale), (w_gate, wg), (w_up, wu),
            )
        )
    ]
    for load in loads:
        load.start()

    steps = sorted({d % ctx_total for j in range(1, STEPS) for d in (j, -j)})
    barrier = pltpu.get_barrier_semaphore()
    for d in steps:
        pl.semaphore_signal(
            barrier, inc=1, device_id={"ctx": lax.rem(ctx + d, ctx_total)}, device_id_type=MESH
        )

    def greet(d):
        pl.semaphore_signal(
            barrier, inc=1, device_id={"exp": lax.rem(me + d, exp_total)}, device_id_type=MESH
        )

    each(1, exp_total, greet)

    loads[1].wait()
    loads[2].wait()
    experts = iota((exp_total, rows), 0)
    named = jnp.zeros((exp_total, rows), F32)
    named_weight = jnp.zeros((exp_total, rows), F32)
    for j in range(IN_FLIGHT):
        hit = (experts == id_rows[j : j + 1, :]).astype(F32)
        named = named + hit
        named_weight = named_weight + hit * weight_rows[j : j + 1, :].astype(F32)
    earlier = (iota((rows, rows), 0) < iota((rows, rows), 1)).astype(BF16)
    rank_send[...] = jnp.where(named > 0.5, dot(named.astype(BF16), earlier), -1.0)
    loads[0].wait()
    pl.semaphore_wait(barrier, exp_total - 1 + len(steps))

    passes = [
        pltpu.make_async_remote_copy(
            src_ref=kv, dst_ref=window.at[j - 1],
            send_sem=kv_send.at[j - 1], recv_sem=kv_recv.at[j - 1],
            device_id={"ctx": lax.rem(ctx + j, ctx_total)}, device_id_type=MESH,
        )
        for j in range(1, STEPS)
    ]
    for one in passes:
        one.start()
    rank_copy = pltpu.make_async_remote_copy(
        src_ref=rank_send, dst_ref=rank_recv, send_sem=rank_sems.at[0],
        recv_sem=rank_sems.at[1], device_id={"exp": across}, device_id_type=MESH,
    )
    rank_copy.start()
    pick[...] = slot_rows(rank_send, base, half, cap, rows)

    own = iota((rows, 1), 0)
    query_pos = positions(ctx, own, rows, ctx_total)
    bias = []
    for j in range(STEPS):
        source = lax.rem(ctx - j + ctx_total, ctx_total)
        key_pos = positions(source, iota((1, rows), 1), rows, ctx_total)
        bias.append(jnp.where(key_pos <= query_pos, 0.0, -1e30))
    bias = jnp.concatenate(bias, axis=1)

    place_row = iota((KVH * HD, WIDE), 0)
    place_lane = lax.rem(iota((KVH * HD, WIDE), 1), HD)
    places = [(place_row == place_lane + g * HD).astype(BF16) for g in range(KVH)]
    lane_head = iota((rows, WIDE), 1) // HD

    def lay_out(g, j):
        block = kv[...] if j == 0 else window[j - 1]
        block_keys = block[:, : KVH * HD] * jnp.asarray(HD ** (-0.5), BF16)
        block_values = block[:, KVH * HD :]
        for part, target in ((block_keys, keys), (block_values, values)):
            tiled = dot(part, places[g])
            for i in range(QUAD):
                at = i * span + j * rows
                target[g, at : at + rows, :] = jnp.where(lane_head == i, tiled, 0.0).astype(BF16)

    lay_out(0, 0)
    loads[3].wait()
    logs_all = jnp.transpose(lse[...])
    loads[4].wait()
    loads[5].wait()
    for j in range(1, STEPS):
        passes[j - 1].wait_recv()
        lay_out(0, j)

    def slots_of(index):
        return pl.ds(pl.multiple_of(index * cap, cap), cap)

    def row_copy(c, to_local, source_ref, sems, source):
        return pltpu.make_async_remote_copy(
            src_ref=source_ref.at[c, slots_of(to_local)],
            dst_ref=recv.at[c, slots_of(source)],
            send_sem=sems.at[c, to_local], recv_sem=row_recv.at[c, source],
            device_id={"exp": base + to_local}, device_id_type=MESH,
        )

    def peer(d):
        return lax.rem(local + d, half)

    def raw_copy(c):
        return pltpu.make_async_remote_copy(
            src_ref=raw.at[c], dst_ref=relay_in.at[c], send_sem=raw_send.at[c],
            recv_sem=raw_recv.at[c], device_id={"exp": across}, device_id_type=MESH,
        )

    def out_copy(c):
        return pltpu.make_async_copy(
            raw.at[c], attended_out.at[:, c * WIDE : (c + 1) * WIDE], out_sem.at[c]
        )

    def meta_copy(to, at):
        return pltpu.make_async_remote_copy(
            src_ref=meta_send.at[to], dst_ref=meta_recv.at[at],
            send_sem=meta_send_sem.at[to], recv_sem=meta_recv_sem.at[at],
            device_id={"exp": to}, device_id_type=MESH,
        )

    def pass_on(c):
        raw_copy(c).wait_recv()
        relay_out[c] = dot(relay_pick[...], relay_in[c]).astype(BF16)
        each(1, half, lambda d: row_copy(c, peer(d), relay_out, relay_send, across).start())
        recv[c, slots_of(across), :] = relay_out[c, slots_of(local), :]

    diagonal = (iota((cap, rows), 0) == iota((cap, rows), 1)).astype(F32)

    def send_weights():
        slot = iota((cap, rows), 0).astype(F32)
        for e in range(exp_total):
            chosen = slot == rank_send[e : e + 1, :]
            column = jnp.sum(
                jnp.where(chosen, named_weight[e : e + 1, :], 0.0), axis=1, keepdims=True
            )
            line = jnp.sum(diagonal * column, axis=0, keepdims=True)
            meta_send[e] = jnp.broadcast_to(line, (8, rows))
        each(1, exp_total, lambda d: meta_copy(lax.rem(me + d, exp_total), me).start())
        meta_recv[me] = meta_send[me]

    def scores_of(c):
        g = c * QUAD // (HQ // KVH)
        return dot(q[:, c * WIDE : (c + 1) * WIDE], keys[g], ((1,), (1,)))

    def absorb(order, c):
        start = (base, far)[order]
        block_rows = pl.ds(pl.multiple_of(start * cap, cap), half * cap)
        each(
            1, half,
            lambda d: row_copy(c, local, send, row_send, start + peer(d)).wait_recv(),
        )
        block = recv[c, block_rows, :].astype(F32)
        square = jnp.sum(block * block, axis=1, keepdims=True)
        lanes = slice(c * WIDE, (c + 1) * WIDE)
        scaled = (block * scale[:, lanes]).astype(BF16)
        gate = dot(scaled, wg[lanes, :])
        up = dot(scaled, wu[lanes, :])
        if c == 0:
            squares[order] = square
            gates[order] = gate
            ups[order] = up
        else:
            squares[order] += square
            gates[order] += gate
            ups[order] += up

    def finish(order):
        start = (base, far)[order]
        each(1, half, lambda d: meta_copy(me, start + peer(d)).wait_recv())
        if order == 1:
            meta_copy(me, across).wait_recv()
        slot_weight = jnp.concatenate(
            [
                jnp.sum(diagonal * meta_recv[start + s][:1, :], axis=1, keepdims=True)
                for s in range(half)
            ],
            axis=0,
        )
        inverse = lax.rsqrt(squares[order] / width + 1e-6)
        gate = gates[order] * inverse
        weight = inverse * slot_weight
        hidden[order] = (gate / (1.0 + jnp.exp(-gate)) * (ups[order] * weight)).astype(BF16)
        block_rows = pl.ds(pl.multiple_of(start * cap, cap), half * cap)
        out = pltpu.make_async_copy(
            hidden.at[order], hidden_out.at[block_rows], local_sem.at[order]
        )
        out.start()
        return out

    heads_per_key = HQ // KVH
    def attend(c, scores):
        lanes = slice(c * WIDE, (c + 1) * WIDE)
        g = c * QUAD // heads_per_key
        powers, carried, total = [], [], []
        for i in range(QUAD):
            part = scores[:, i * span : (i + 1) * span] + bias
            head = c * QUAD + i
            logs = logs_all[:, head : head + 1]
            row_max = jnp.maximum(jnp.max(part, axis=1, keepdims=True), logs)
            power = jnp.exp(part - row_max)
            share = jnp.exp(logs - row_max)
            carried.append(share)
            total.append(share + jnp.sum(power, axis=1, keepdims=True))
            powers.append(power.astype(BF16))
        mixed = dot(jnp.concatenate(powers, axis=1), values[g])
        result = (
            spread(carried, rows) * prior[:, lanes].astype(F32) + mixed
        ) / spread(total, rows)
        result = result.astype(BF16)
        raw[c] = result
        raw_copy(c).start()
        send[c] = dot(pick[...], result).astype(BF16)
        each(1, half, lambda d: row_copy(c, peer(d), send, row_send, me).start())
        out_copy(c).start()
        recv[c, slots_of(me), :] = send[c, slots_of(local), :]

    lag, near_lag, far_lag = 2, 3, 5
    ahead = scores_of(0)
    for c in range(chunks + far_lag):
        if c < chunks:
            scores = ahead
            if c + 1 < chunks:
                if (c + 1) * QUAD % heads_per_key == 0:
                    for j in range(STEPS):
                        lay_out((c + 1) * QUAD // heads_per_key, j)
                ahead = scores_of(c + 1)
            attend(c, scores)
        if c == 0:
            rank_copy.wait_recv()
            relay_pick[...] = slot_rows(rank_recv, base, half, cap, rows)
        if c == 1:
            send_weights()
        if 0 <= c - lag < chunks:
            pass_on(c - lag)
        if c == near_lag:
            loads[6].wait()
            loads[7].wait()
            loads[8].wait()
        if 0 <= c - near_lag < chunks:
            absorb(0, c - near_lag)
        if c - near_lag == chunks - 1:
            stores = [finish(0)]
        if 0 <= c - far_lag < chunks:
            absorb(1, c - far_lag)
    stores.append(finish(1))

    for one in passes:
        one.wait_send()
    rank_copy.wait_send()
    each(1, exp_total, lambda d: meta_copy(lax.rem(me + d, exp_total), me).wait_send())
    for c in range(chunks):
        raw_copy(c).wait_send()
        out_copy(c).wait()

    def sent(d):
        for c in range(chunks):
            row_copy(c, peer(d), send, row_send, me).wait_send()
            row_copy(c, peer(d), relay_out, relay_send, across).wait_send()

    each(1, half, sent)
    for out in stores:
        out.wait()


def hand_over(attended, hidden, attended_out, hidden_out, sems):
    copies = []
    for k, (source, target) in enumerate(((attended, attended_out), (hidden, hidden_out))):
        step = source.shape[0] // PIECES
        for i in range(PIECES):
            part = pl.ds(i * step, step)
            copies.append(
                pltpu.make_async_copy(source.at[part], target.at[part], sems.at[k, i])
            )
    for one in copies:
        one.start()
    for one in copies:
        one.wait()


def per_device(
    query, key_value, prior_out, prior_lse, norm_gain, w_gate, w_up, expert_ids, route_weight
):
    ctx_total = lax.axis_size("ctx")
    exp_total = lax.axis_size("exp")
    rows, width = query.shape[1:]
    hidden_width = w_gate.shape[2]
    capacity = max(2, IN_FLIGHT * rows * 3 // (2 * exp_total))
    cap = -(-capacity // 16) * 16
    chunks = width // WIDE
    pair_width = key_value.shape[2]
    any_space = pl.BlockSpec(memory_space=pl.ANY)
    dma = pltpu.SemaphoreType.DMA
    slots = exp_total * cap
    half_slots = exp_total // 2 * cap
    attended, hidden = pl.pallas_call(
        functools.partial(kernel, ctx_total, exp_total, cap),
        out_shape=(
            jax.ShapeDtypeStruct((rows, width), BF16),
            jax.ShapeDtypeStruct((slots, hidden_width), BF16),
        ),
        in_specs=[any_space] * 9,
        out_specs=(any_space, any_space),
        scratch_shapes=[
            pltpu.VMEM((rows, width), BF16),
            pltpu.VMEM((rows, pair_width), BF16),
            pltpu.VMEM((rows, width), BF16),
            pltpu.VMEM((HQ, rows), F32),
            pltpu.VMEM((1, width), F32),
            pltpu.VMEM(w_gate.shape[1:], BF16),
            pltpu.VMEM(w_up.shape[1:], BF16),
            pltpu.VMEM((IN_FLIGHT, rows), jnp.int32),
            pltpu.VMEM((IN_FLIGHT, rows), BF16),
            pltpu.VMEM((STEPS - 1, rows, pair_width), BF16),
            pltpu.VMEM((KVH, QUAD * STEPS * rows, WIDE), BF16),
            pltpu.VMEM((KVH, QUAD * STEPS * rows, WIDE), BF16),
            pltpu.VMEM((chunks, rows, WIDE), BF16),
            pltpu.VMEM((half_slots, rows), BF16),
            pltpu.VMEM((half_slots, rows), BF16),
            pltpu.VMEM((chunks, half_slots, WIDE), BF16),
            pltpu.VMEM((chunks, rows, WIDE), BF16),
            pltpu.VMEM((chunks, half_slots, WIDE), BF16),
            pltpu.VMEM((chunks, slots, WIDE), BF16),
            pltpu.VMEM((exp_total, rows), F32),
            pltpu.VMEM((exp_total, rows), F32),
            pltpu.VMEM((exp_total, 8, rows), F32),
            pltpu.VMEM((exp_total, 8, rows), F32),
            pltpu.VMEM((2, half_slots, 1), F32),
            pltpu.VMEM((2, half_slots, hidden_width), F32),
            pltpu.VMEM((2, half_slots, hidden_width), F32),
            pltpu.VMEM((2, half_slots, hidden_width), BF16),
            dma((9,)),
            dma((chunks,)),
            dma((STEPS - 1,)),
            dma((STEPS - 1,)),
            dma((chunks, exp_total // 2)),
            dma((chunks, exp_total)),
            dma((chunks, exp_total // 2)),
            dma((chunks,)),
            dma((chunks,)),
            dma((2,)),
            dma((exp_total,)),
            dma((exp_total,)),
        ],
        compiler_params=pltpu.CompilerParams(
            collective_id=0, has_side_effects=True, vmem_limit_bytes=60 * 1024 * 1024
        ),
    )(
        query[0], key_value[0], prior_out[0], prior_lse[0].T, norm_gain[None], w_gate[0], w_up[0],
        expert_ids[0].T, route_weight[0].T,
    )
    attended, hidden = pl.pallas_call(
        hand_over,
        out_shape=(
            jax.ShapeDtypeStruct((rows, width), BF16),
            jax.ShapeDtypeStruct((slots, hidden_width), BF16),
        ),
        in_specs=[any_space] * 2,
        out_specs=(any_space, any_space),
        scratch_shapes=[dma((2, PIECES))],
        compiler_params=pltpu.CompilerParams(vmem_limit_bytes=60 * 1024 * 1024),
    )(attended, hidden)
    hidden = hidden.reshape(exp_total, cap, hidden_width)[:, :capacity]
    return (attended[None], hidden.reshape(1, 1, exp_total * capacity, hidden_width))


def solution(mesh):
    placed = (
        P("exp", "ctx", None),
        P("exp", "ctx", None),
        P("exp", "ctx", None),
        P("exp", "ctx", None),
        P(),
        P("exp", None, None),
        P("exp", None, None),
        P("exp", "ctx", None),
        P("exp", "ctx", None),
    )
    return jax.shard_map(
        per_device,
        mesh=mesh,
        in_specs=placed,
        out_specs=(P("exp", "ctx", None), P("ctx", "exp", None, None)),
        check_vma=False,
    )
```

```python
import functools

import jax
import jax.numpy as jnp
from jax import lax
from jax.experimental import pallas as pl
from jax.experimental.pallas import tpu as pltpu
from jax.sharding import PartitionSpec as P

HQ = 32
KVH = 2
HD = 64
FF = 768
STEPS = 3
IN_FLIGHT = 2

MESH = pl.DeviceIdType.MESH
WIDE = 256
QUAD = WIDE // HD
PIECES = 4
F32 = jnp.float32
BF16 = jnp.bfloat16


def dot(a, b, contract=((1,), (0,))):
    return lax.dot_general(a, b, (contract, ((), ())), preferred_element_type=F32)


def iota(shape, dim):
    return lax.broadcasted_iota(jnp.int32, shape, dim)


def positions(block, offset, rows, total):
    half = rows // 2
    return jnp.where(
        offset < half, block * half + offset, (2 * total - 1 - block) * half + offset - half
    )


def each(first, last, body):
    if last - first <= 8:
        for d in range(first, last):
            body(d)
    else:
        lax.fori_loop(first, last, lambda d, _: (body(d), 0)[1], 0)


def slot_rows(rank_ref, base, count, cap, rows):
    slot = iota((cap, rows), 0).astype(F32)
    return jnp.concatenate(
        [(slot == rank_ref[pl.ds(base + e, 1), :]).astype(BF16) for e in range(count)], axis=0
    )


def kernel(
    ctx_total, exp_total, cap,
    query, key_value, prior_out, prior_lse, gain, w_gate, w_up, ids, weights,
    attended_out, hidden_out,
    q, kv, prior, lse, scale, wg, wu, id_rows, weight_rows,
    window, keys, values, raw, pick, relay_pick, send, relay_in, relay_out, recv,
    rank_send, rank_recv, meta_send, meta_recv, squares, gates, ups, hidden,
    local_sem, out_sem, kv_send, kv_recv, row_send, row_recv, relay_send,
    raw_send, raw_recv, rank_sems, meta_send_sem, meta_recv_sem,
):
    rows = q.shape[0]
    width = q.shape[1]
    chunks = width // WIDE
    half = exp_total // 2
    me = lax.axis_index("exp")
    ctx = lax.axis_index("ctx")
    side = me // half
    base = side * half
    local = me - base
    far = half - base
    across = lax.rem(me + half, exp_total)

    loads = [
        pltpu.make_async_copy(a, b, local_sem.at[i])
        for i, (a, b) in enumerate(
            (
                (key_value, kv), (ids, id_rows), (weights, weight_rows), (prior_lse, lse),
                (query, q), (prior_out, prior), (gain, scale), (w_gate, wg), (w_up, wu),
            )
        )
    ]
    for load in loads:
        load.start()

    steps = sorted({d % ctx_total for j in range(1, STEPS) for d in (j, -j)})
    barrier = pltpu.get_barrier_semaphore()
    for d in steps:
        pl.semaphore_signal(
            barrier, inc=1, device_id={"ctx": lax.rem(ctx + d, ctx_total)}, device_id_type=MESH
        )

    def greet(d):
        pl.semaphore_signal(
            barrier, inc=1, device_id={"exp": lax.rem(me + d, exp_total)}, device_id_type=MESH
        )

    each(1, exp_total, greet)

    loads[1].wait()
    loads[2].wait()
    experts = iota((exp_total, rows), 0)
    named = jnp.zeros((exp_total, rows), F32)
    named_weight = jnp.zeros((exp_total, rows), F32)
    for j in range(IN_FLIGHT):
        hit = (experts == id_rows[j : j + 1, :]).astype(F32)
        named = named + hit
        named_weight = named_weight + hit * weight_rows[j : j + 1, :].astype(F32)
    earlier = (iota((rows, rows), 0) < iota((rows, rows), 1)).astype(BF16)
    rank_send[...] = jnp.where(named > 0.5, dot(named.astype(BF16), earlier), -1.0)
    loads[0].wait()
    pl.semaphore_wait(barrier, exp_total - 1 + len(steps))

    passes = [
        pltpu.make_async_remote_copy(
            src_ref=kv, dst_ref=window.at[j - 1],
            send_sem=kv_send.at[j - 1], recv_sem=kv_recv.at[j - 1],
            device_id={"ctx": lax.rem(ctx + j, ctx_total)}, device_id_type=MESH,
        )
        for j in range(1, STEPS)
    ]
    for one in passes:
        one.start()
    rank_copy = pltpu.make_async_remote_copy(
        src_ref=rank_send, dst_ref=rank_recv, send_sem=rank_sems.at[0],
        recv_sem=rank_sems.at[1], device_id={"exp": across}, device_id_type=MESH,
    )
    rank_copy.start()
    pick[...] = slot_rows(rank_send, base, half, cap, rows)

    own = iota((rows, 1), 0)
    query_pos = positions(ctx, own, rows, ctx_total)
    bias = []
    for j in range(STEPS):
        source = lax.rem(ctx - j + ctx_total, ctx_total)
        key_pos = positions(source, iota((1, rows), 1), rows, ctx_total)
        bias.append(jnp.where(key_pos <= query_pos, 0.0, -1e30))
    bias = jnp.concatenate(bias, axis=1)
    bias = jnp.concatenate([bias] * QUAD, axis=0)

    place_row = iota((KVH * HD, WIDE), 0)
    place_lane = iota((KVH * HD, WIDE), 1)
    lane_head = iota((rows, WIDE), 1) // HD
    lane = iota((rows, WIDE // 2), 1)

    def lay_out(j):
        block = kv[...] if j == 0 else window[j - 1]
        block_keys = block[:, : KVH * HD] * jnp.asarray(HD ** (-0.5), BF16)
        block_values = block[:, KVH * HD :]
        at = slice(j * rows, (j + 1) * rows)
        for g in range(KVH):
            place = (place_row == lax.rem(place_lane, HD) + g * HD).astype(BF16)
            keys[g, at, :] = dot(block_keys, place).astype(BF16)
            tiled = dot(block_values, place)
            values[g, at, :] = jnp.where(lane_head < QUAD // 2, tiled, 1.0).astype(BF16)

    lay_out(0)
    loads[3].wait()
    logs_all = jnp.transpose(lse[...])
    loads[4].wait()
    loads[5].wait()
    for j in range(1, STEPS):
        passes[j - 1].wait_recv()
        lay_out(j)

    def slots_of(index):
        return pl.ds(pl.multiple_of(index * cap, cap), cap)

    def row_copy(c, to_local, source_ref, sems, source):
        return pltpu.make_async_remote_copy(
            src_ref=source_ref.at[c, slots_of(to_local)],
            dst_ref=recv.at[c, slots_of(source)],
            send_sem=sems.at[c, to_local], recv_sem=row_recv.at[c, source],
            device_id={"exp": base + to_local}, device_id_type=MESH,
        )

    def peer(d):
        return lax.rem(local + d, half)

    def raw_copy(c):
        return pltpu.make_async_remote_copy(
            src_ref=raw.at[c], dst_ref=relay_in.at[c], send_sem=raw_send.at[c],
            recv_sem=raw_recv.at[c], device_id={"exp": across}, device_id_type=MESH,
        )

    def out_copy(c):
        return pltpu.make_async_copy(
            raw.at[c], attended_out.at[:, c * WIDE : (c + 1) * WIDE], out_sem.at[c]
        )

    def meta_copy(to, at):
        return pltpu.make_async_remote_copy(
            src_ref=meta_send.at[to], dst_ref=meta_recv.at[at],
            send_sem=meta_send_sem.at[to], recv_sem=meta_recv_sem.at[at],
            device_id={"exp": to}, device_id_type=MESH,
        )

    def pass_on(c):
        raw_copy(c).wait_recv()
        relay_out[c] = dot(relay_pick[...], relay_in[c]).astype(BF16)
        each(1, half, lambda d: row_copy(c, peer(d), relay_out, relay_send, across).start())
        recv[c, slots_of(across), :] = relay_out[c, slots_of(local), :]

    diagonal = (iota((cap, rows), 0) == iota((cap, rows), 1)).astype(F32)

    def send_weights():
        slot = iota((cap, rows), 0).astype(F32)
        for e in range(exp_total):
            chosen = slot == rank_send[e : e + 1, :]
            column = jnp.sum(
                jnp.where(chosen, named_weight[e : e + 1, :], 0.0), axis=1, keepdims=True
            )
            line = jnp.sum(diagonal * column, axis=0, keepdims=True)
            meta_send[e] = jnp.broadcast_to(line, (8, rows))
        each(1, exp_total, lambda d: meta_copy(lax.rem(me + d, exp_total), me).start())
        meta_recv[me] = meta_send[me]

    def scores_of(c):
        g = c * QUAD // heads_per_key
        four = q[:, c * WIDE : (c + 1) * WIDE]
        none = jnp.zeros((), BF16)
        stacked = jnp.concatenate(
            [jnp.where(lane_head == i, four, none) for i in range(QUAD)], axis=0
        )
        return dot(stacked, keys[g], ((1,), (1,))) + bias

    def by_pair(parts, lanes):
        return jnp.concatenate(
            [
                jnp.where(
                    lane < HD,
                    parts[p * rows : (p + 1) * rows, lanes],
                    parts[(p + 1) * rows : (p + 2) * rows, lanes],
                )
                for p in range(0, QUAD, 2)
            ],
            axis=1,
        )

    def absorb(order, c):
        start = (base, far)[order]
        block_rows = pl.ds(pl.multiple_of(start * cap, cap), half * cap)
        each(
            1, half,
            lambda d: row_copy(c, local, send, row_send, start + peer(d)).wait_recv(),
        )
        block = recv[c, block_rows, :].astype(F32)
        square = jnp.sum(block * block, axis=1, keepdims=True)
        lanes = slice(c * WIDE, (c + 1) * WIDE)
        scaled = (block * scale[:, lanes]).astype(BF16)
        gate = dot(scaled, wg[lanes, :])
        up = dot(scaled, wu[lanes, :])
        if c == 0:
            squares[order] = square
            gates[order] = gate
            ups[order] = up
        else:
            squares[order] += square
            gates[order] += gate
            ups[order] += up

    def finish(order):
        start = (base, far)[order]
        each(1, half, lambda d: meta_copy(me, start + peer(d)).wait_recv())
        if order == 1:
            meta_copy(me, across).wait_recv()
        slot_weight = jnp.concatenate(
            [
                jnp.sum(diagonal * meta_recv[start + s][:1, :], axis=1, keepdims=True)
                for s in range(half)
            ],
            axis=0,
        )
        inverse = lax.rsqrt(squares[order] / width + 1e-6)
        gate = gates[order] * inverse
        weight = inverse * slot_weight
        hidden[order] = (gate / (1.0 + jnp.exp(-gate)) * (ups[order] * weight)).astype(BF16)
        block_rows = pl.ds(pl.multiple_of(start * cap, cap), half * cap)
        out = pltpu.make_async_copy(
            hidden.at[order], hidden_out.at[block_rows], local_sem.at[order]
        )
        out.start()
        return out

    heads_per_key = HQ // KVH
    def attend(c, scores):
        lanes = slice(c * WIDE, (c + 1) * WIDE)
        logs = jnp.concatenate(
            [logs_all[:, c * QUAD + i : c * QUAD + i + 1] for i in range(QUAD)], axis=0
        )
        row_max = jnp.maximum(jnp.max(scores, axis=1, keepdims=True), logs)
        powers = jnp.exp(scores - row_max).astype(BF16)
        carried = by_pair(
            jnp.broadcast_to(jnp.exp(logs - row_max), (QUAD * rows, WIDE // 2)),
            slice(0, WIDE // 2),
        )
        mixed = dot(powers, values[c * QUAD // heads_per_key])
        total = carried + by_pair(mixed, slice(WIDE // 2, WIDE))
        result = (
            carried * prior[:, lanes].astype(F32) + by_pair(mixed, slice(0, WIDE // 2))
        ) / total
        result = result.astype(BF16)
        raw[c] = result
        raw_copy(c).start()
        send[c] = dot(pick[...], result).astype(BF16)
        each(1, half, lambda d: row_copy(c, peer(d), send, row_send, me).start())
        out_copy(c).start()
        recv[c, slots_of(me), :] = send[c, slots_of(local), :]

    lag, near_lag, far_lag = 2, 3, 5
    ahead = scores_of(0)
    for c in range(chunks + far_lag):
        if c < chunks:
            scores = ahead
            if c + 1 < chunks:
                ahead = scores_of(c + 1)
            attend(c, scores)
        if c == 0:
            rank_copy.wait_recv()
            relay_pick[...] = slot_rows(rank_recv, base, half, cap, rows)
        if c == 1:
            send_weights()
        if 0 <= c - lag < chunks:
            pass_on(c - lag)
        if c == near_lag:
            loads[6].wait()
            loads[7].wait()
            loads[8].wait()
        if 0 <= c - near_lag < chunks:
            absorb(0, c - near_lag)
        if c - near_lag == chunks - 1:
            stores = [finish(0)]
        if 0 <= c - far_lag < chunks:
            absorb(1, c - far_lag)
    stores.append(finish(1))

    for one in passes:
        one.wait_send()
    rank_copy.wait_send()
    each(1, exp_total, lambda d: meta_copy(lax.rem(me + d, exp_total), me).wait_send())
    for c in range(chunks):
        raw_copy(c).wait_send()
        out_copy(c).wait()

    def sent(d):
        for c in range(chunks):
            row_copy(c, peer(d), send, row_send, me).wait_send()
            row_copy(c, peer(d), relay_out, relay_send, across).wait_send()

    each(1, half, sent)
    for out in stores:
        out.wait()


def hand_over(attended, hidden, attended_out, hidden_out, rows_held, hidden_held, sems):
    fetches, stores = [], []
    pairs = ((attended, rows_held, attended_out), (hidden, hidden_held, hidden_out))
    for k, (source, held, target) in enumerate(pairs):
        step = source.shape[0] // PIECES
        for i in range(PIECES):
            part = pl.ds(i * step, step)
            fetches.append(pltpu.make_async_copy(source.at[part], held.at[part], sems.at[0, k, i]))
            stores.append(pltpu.make_async_copy(held.at[part], target.at[part], sems.at[1, k, i]))
    for fetch in fetches:
        fetch.start()
    for fetch, store in zip(fetches, stores):
        fetch.wait()
        store.start()
    for store in stores:
        store.wait()


def per_device(
    query, key_value, prior_out, prior_lse, norm_gain, w_gate, w_up, expert_ids, route_weight
):
    ctx_total = lax.axis_size("ctx")
    exp_total = lax.axis_size("exp")
    rows, width = query.shape[1:]
    hidden_width = w_gate.shape[2]
    capacity = max(2, IN_FLIGHT * rows * 3 // (2 * exp_total))
    cap = -(-capacity // 16) * 16
    chunks = width // WIDE
    pair_width = key_value.shape[2]
    any_space = pl.BlockSpec(memory_space=pl.ANY)
    dma = pltpu.SemaphoreType.DMA
    slots = exp_total * cap
    half_slots = exp_total // 2 * cap
    attended, hidden = pl.pallas_call(
        functools.partial(kernel, ctx_total, exp_total, cap),
        out_shape=(
            jax.ShapeDtypeStruct((rows, width), BF16),
            jax.ShapeDtypeStruct((slots, hidden_width), BF16),
        ),
        in_specs=[any_space] * 9,
        out_specs=(any_space, any_space),
        scratch_shapes=[
            pltpu.VMEM((rows, width), BF16),
            pltpu.VMEM((rows, pair_width), BF16),
            pltpu.VMEM((rows, width), BF16),
            pltpu.VMEM((HQ, rows), F32),
            pltpu.VMEM((1, width), F32),
            pltpu.VMEM(w_gate.shape[1:], BF16),
            pltpu.VMEM(w_up.shape[1:], BF16),
            pltpu.VMEM((IN_FLIGHT, rows), jnp.int32),
            pltpu.VMEM((IN_FLIGHT, rows), BF16),
            pltpu.VMEM((STEPS - 1, rows, pair_width), BF16),
            pltpu.VMEM((KVH, STEPS * rows, WIDE), BF16),
            pltpu.VMEM((KVH, STEPS * rows, WIDE), BF16),
            pltpu.VMEM((chunks, rows, WIDE), BF16),
            pltpu.VMEM((half_slots, rows), BF16),
            pltpu.VMEM((half_slots, rows), BF16),
            pltpu.VMEM((chunks, half_slots, WIDE), BF16),
            pltpu.VMEM((chunks, rows, WIDE), BF16),
            pltpu.VMEM((chunks, half_slots, WIDE), BF16),
            pltpu.VMEM((chunks, slots, WIDE), BF16),
            pltpu.VMEM((exp_total, rows), F32),
            pltpu.VMEM((exp_total, rows), F32),
            pltpu.VMEM((exp_total, 8, rows), F32),
            pltpu.VMEM((exp_total, 8, rows), F32),
            pltpu.VMEM((2, half_slots, 1), F32),
            pltpu.VMEM((2, half_slots, hidden_width), F32),
            pltpu.VMEM((2, half_slots, hidden_width), F32),
            pltpu.VMEM((2, half_slots, hidden_width), BF16),
            dma((9,)),
            dma((chunks,)),
            dma((STEPS - 1,)),
            dma((STEPS - 1,)),
            dma((chunks, exp_total // 2)),
            dma((chunks, exp_total)),
            dma((chunks, exp_total // 2)),
            dma((chunks,)),
            dma((chunks,)),
            dma((2,)),
            dma((exp_total,)),
            dma((exp_total,)),
        ],
        compiler_params=pltpu.CompilerParams(
            collective_id=0, has_side_effects=True, vmem_limit_bytes=60 * 1024 * 1024
        ),
    )(
        query[0], key_value[0], prior_out[0], prior_lse[0].T, norm_gain[None], w_gate[0], w_up[0],
        expert_ids[0].T, route_weight[0].T,
    )
    attended, hidden = pl.pallas_call(
        hand_over,
        out_shape=(
            jax.ShapeDtypeStruct((rows, width), BF16),
            jax.ShapeDtypeStruct((slots, hidden_width), BF16),
        ),
        in_specs=[any_space] * 2,
        out_specs=(any_space, any_space),
        scratch_shapes=[
            pltpu.VMEM((rows, width), BF16),
            pltpu.VMEM((slots, hidden_width), BF16),
            dma((2, 2, PIECES)),
        ],
        compiler_params=pltpu.CompilerParams(vmem_limit_bytes=60 * 1024 * 1024),
    )(attended, hidden)
    hidden = hidden.reshape(exp_total, cap, hidden_width)[:, :capacity]
    return (attended[None], hidden.reshape(1, 1, exp_total * capacity, hidden_width))


def solution(mesh):
    placed = (
        P("exp", "ctx", None),
        P("exp", "ctx", None),
        P("exp", "ctx", None),
        P("exp", "ctx", None),
        P(),
        P("exp", None, None),
        P("exp", None, None),
        P("exp", "ctx", None),
        P("exp", "ctx", None),
    )
    return jax.shard_map(
        per_device,
        mesh=mesh,
        in_specs=placed,
        out_specs=(P("exp", "ctx", None), P("ctx", "exp", None, None)),
        check_vma=False,
    )
```

```python
import functools

import jax
import jax.numpy as jnp
from jax import lax
from jax.experimental import pallas as pl
from jax.experimental.pallas import tpu as pltpu
from jax.sharding import PartitionSpec as P

HQ = 32
KVH = 2
HD = 64
FF = 768
STEPS = 3
IN_FLIGHT = 2

MESH = pl.DeviceIdType.MESH
WIDE = 256
QUAD = WIDE // HD
PIECES = 4
CORES = 2
F32 = jnp.float32
BF16 = jnp.bfloat16


def dot(a, b, contract=((1,), (0,))):
    return lax.dot_general(a, b, (contract, ((), ())), preferred_element_type=F32)


def iota(shape, dim):
    return lax.broadcasted_iota(jnp.int32, shape, dim)


def positions(block, offset, rows, total):
    half = rows // 2
    return jnp.where(
        offset < half, block * half + offset, (2 * total - 1 - block) * half + offset - half
    )


def each(first, last, body):
    if last - first <= 8:
        for d in range(first, last):
            body(d)
    else:
        lax.fori_loop(first, last, lambda d, _: (body(d), 0)[1], 0)


def slot_rows(rank_ref, base, count, cap, rows):
    slot = iota((cap, rows), 0).astype(F32)
    return jnp.concatenate(
        [(slot == rank_ref[pl.ds(base + e, 1), :]).astype(BF16) for e in range(count)], axis=0
    )


def kernel(
    ctx_total, exp_total, cap, share,
    query, key_value, prior_out, prior_lse, gain, w_gate, w_up, ids, weights,
    attended_out, hidden_out,
    q, kv, prior, lse, scale, wg, wu, id_rows, weight_rows,
    window, keys, values, raw, pick, relay_pick, send, relay_in, relay_out, recv,
    rank_send, rank_recv, meta_send, meta_recv, squares, gates, ups, hidden,
    local_sem, out_sem, kv_send, kv_recv, row_send, row_recv, relay_send,
    raw_send, raw_recv, rank_sems, meta_send_sem, meta_recv_sem,
):
    rows = q.shape[0]
    width = q.shape[1]
    chunks = width // WIDE
    half = exp_total // 2
    me = lax.axis_index("exp")
    ctx = lax.axis_index("ctx")
    side = me // half
    base = side * half
    local = me - base
    far = half - base
    paired = share > 1
    core = lax.rem(me, CORES)
    if paired:
        across = half + core - CORES * side
        passes_on = me == half + core - CORES * (1 - side)
        place = local // CORES
        served = [far + core + CORES * k for k in range(share)]
    else:
        across = lax.rem(me + half, exp_total)
        passes_on = None
        place = 0
        served = [across]

    def if_passing(body):
        if paired:
            pl.when(passes_on)(body)
        else:
            body()


    loads = [
        pltpu.make_async_copy(a, b, local_sem.at[i])
        for i, (a, b) in enumerate(
            (
                (key_value, kv), (ids, id_rows), (weights, weight_rows), (prior_lse, lse),
                (query, q), (prior_out, prior), (gain, scale), (w_gate, wg), (w_up, wu),
            )
        )
    ]
    for load in loads:
        load.start()

    steps = sorted({d % ctx_total for j in range(1, STEPS) for d in (j, -j)})
    barrier = pltpu.get_barrier_semaphore()
    for d in steps:
        pl.semaphore_signal(
            barrier, inc=1, device_id={"ctx": lax.rem(ctx + d, ctx_total)}, device_id_type=MESH
        )

    def greet(d):
        pl.semaphore_signal(
            barrier, inc=1, device_id={"exp": lax.rem(me + d, exp_total)}, device_id_type=MESH
        )

    each(1, exp_total, greet)

    loads[1].wait()
    loads[2].wait()
    experts = iota((exp_total, rows), 0)
    named = jnp.zeros((exp_total, rows), F32)
    named_weight = jnp.zeros((exp_total, rows), F32)
    for j in range(IN_FLIGHT):
        hit = (experts == id_rows[j : j + 1, :]).astype(F32)
        named = named + hit
        named_weight = named_weight + hit * weight_rows[j : j + 1, :].astype(F32)
    earlier = (iota((rows, rows), 0) < iota((rows, rows), 1)).astype(BF16)
    rank_send[...] = jnp.where(named > 0.5, dot(named.astype(BF16), earlier), -1.0)
    loads[0].wait()
    pl.semaphore_wait(barrier, exp_total - 1 + len(steps))

    passes = [
        pltpu.make_async_remote_copy(
            src_ref=kv, dst_ref=window.at[j - 1],
            send_sem=kv_send.at[j - 1], recv_sem=kv_recv.at[j - 1],
            device_id={"ctx": lax.rem(ctx + j, ctx_total)}, device_id_type=MESH,
        )
        for j in range(1, STEPS)
    ]
    for one in passes:
        one.start()
    rank_copy = pltpu.make_async_remote_copy(
        src_ref=rank_send, dst_ref=rank_recv.at[place], send_sem=rank_sems.at[share],
        recv_sem=rank_sems.at[place], device_id={"exp": across}, device_id_type=MESH,
    )
    rank_copy.start()
    pick[...] = slot_rows(rank_send, base, half, cap, rows)

    own = iota((rows, 1), 0)
    query_pos = positions(ctx, own, rows, ctx_total)
    bias = []
    for j in range(STEPS):
        source = lax.rem(ctx - j + ctx_total, ctx_total)
        key_pos = positions(source, iota((1, rows), 1), rows, ctx_total)
        bias.append(jnp.where(key_pos <= query_pos, 0.0, -1e30))
    bias = jnp.concatenate(bias, axis=1)
    bias = jnp.concatenate([bias] * QUAD, axis=0)

    place_row = iota((KVH * HD, WIDE), 0)
    place_lane = iota((KVH * HD, WIDE), 1)
    lane_head = iota((rows, WIDE), 1) // HD
    lane = iota((rows, WIDE // 2), 1)

    def lay_out(j):
        block = kv[...] if j == 0 else window[j - 1]
        block_keys = block[:, : KVH * HD] * jnp.asarray(HD ** (-0.5), BF16)
        block_values = block[:, KVH * HD :]
        at = slice(j * rows, (j + 1) * rows)
        for g in range(KVH):
            place = (place_row == lax.rem(place_lane, HD) + g * HD).astype(BF16)
            keys[g, at, :] = dot(block_keys, place).astype(BF16)
            tiled = dot(block_values, place)
            values[g, at, :] = jnp.where(lane_head < QUAD // 2, tiled, 1.0).astype(BF16)

    lay_out(0)
    loads[3].wait()
    logs_all = jnp.transpose(lse[...])
    loads[4].wait()
    loads[5].wait()
    for j in range(1, STEPS):
        passes[j - 1].wait_recv()
        lay_out(j)

    def slots_of(index):
        return pl.ds(pl.multiple_of(index * cap, cap), cap)

    def row_copy(c, to_local, source_ref, sems, source):
        return pltpu.make_async_remote_copy(
            src_ref=source_ref.at[c, slots_of(to_local)],
            dst_ref=recv.at[c, slots_of(source)],
            send_sem=sems.at[c, to_local], recv_sem=row_recv.at[c, source],
            device_id={"exp": base + to_local}, device_id_type=MESH,
        )

    def peer(d):
        return lax.rem(local + d, half)

    def raw_copy(c):
        return pltpu.make_async_remote_copy(
            src_ref=raw.at[c], dst_ref=relay_in.at[c, place], send_sem=raw_send.at[c],
            recv_sem=raw_recv.at[c, place], device_id={"exp": across}, device_id_type=MESH,
        )

    def out_copy(c):
        return pltpu.make_async_copy(
            raw.at[c], attended_out.at[:, c * WIDE : (c + 1) * WIDE], out_sem.at[c]
        )

    def meta_copy(to, at):
        return pltpu.make_async_remote_copy(
            src_ref=meta_send.at[to], dst_ref=meta_recv.at[at],
            send_sem=meta_send_sem.at[to], recv_sem=meta_recv_sem.at[at],
            device_id={"exp": to}, device_id_type=MESH,
        )

    def relay_copy(c, k, to_local):
        return pltpu.make_async_remote_copy(
            src_ref=relay_out.at[c, k, slots_of(to_local)],
            dst_ref=recv.at[c, slots_of(served[k])],
            send_sem=relay_send.at[c, k, to_local], recv_sem=row_recv.at[c, served[k]],
            device_id={"exp": base + to_local}, device_id_type=MESH,
        )

    def pass_on(c):
        for k in range(share):
            pltpu.make_async_remote_copy(
                src_ref=raw.at[c], dst_ref=relay_in.at[c, k], send_sem=raw_send.at[c],
                recv_sem=raw_recv.at[c, k], device_id={"exp": across}, device_id_type=MESH,
            ).wait_recv()
            relay_out[c, k] = dot(relay_pick[k], relay_in[c, k]).astype(BF16)
            each(1, half, lambda d, k=k: relay_copy(c, k, peer(d)).start())
            recv[c, slots_of(served[k]), :] = relay_out[c, k, slots_of(local), :]

    def ready():
        for k in range(share):
            pltpu.make_async_remote_copy(
                src_ref=rank_send, dst_ref=rank_recv.at[k], send_sem=rank_sems.at[share],
                recv_sem=rank_sems.at[k], device_id={"exp": across}, device_id_type=MESH,
            ).wait_recv()
            relay_pick[k] = slot_rows(rank_recv.at[k], base, half, cap, rows)

    diagonal = (iota((cap, rows), 0) == iota((cap, rows), 1)).astype(F32)

    def send_weights():
        slot = iota((cap, rows), 0).astype(F32)
        for e in range(exp_total):
            chosen = slot == rank_send[e : e + 1, :]
            column = jnp.sum(
                jnp.where(chosen, named_weight[e : e + 1, :], 0.0), axis=1, keepdims=True
            )
            line = jnp.sum(diagonal * column, axis=0, keepdims=True)
            meta_send[e] = jnp.broadcast_to(line, (8, rows))
        each(1, exp_total, lambda d: meta_copy(lax.rem(me + d, exp_total), me).start())
        meta_recv[me] = meta_send[me]

    def scores_of(c):
        g = c * QUAD // heads_per_key
        four = q[:, c * WIDE : (c + 1) * WIDE]
        none = jnp.zeros((), BF16)
        stacked = jnp.concatenate(
            [jnp.where(lane_head == i, four, none) for i in range(QUAD)], axis=0
        )
        return dot(stacked, keys[g], ((1,), (1,))) + bias

    def by_pair(parts, lanes):
        return jnp.concatenate(
            [
                jnp.where(
                    lane < HD,
                    parts[p * rows : (p + 1) * rows, lanes],
                    parts[(p + 1) * rows : (p + 2) * rows, lanes],
                )
                for p in range(0, QUAD, 2)
            ],
            axis=1,
        )

    def absorb(order, c):
        start = (base, far)[order]
        block_rows = pl.ds(pl.multiple_of(start * cap, cap), half * cap)
        if order == 1 and paired:
            for k in range(share):
                row_copy(c, local, send, row_send, far + 1 - core + CORES * k).wait_recv()

            @pl.when(jnp.logical_not(passes_on))
            def _():
                for k in range(share):
                    row_copy(c, local, send, row_send, served[k]).wait_recv()
        else:
            each(
                1, half,
                lambda d: row_copy(c, local, send, row_send, start + peer(d)).wait_recv(),
            )
        block = recv[c, block_rows, :].astype(F32)
        square = jnp.sum(block * block, axis=1, keepdims=True)
        lanes = slice(c * WIDE, (c + 1) * WIDE)
        scaled = (block * scale[:, lanes]).astype(BF16)
        gate = dot(scaled, wg[lanes, :])
        up = dot(scaled, wu[lanes, :])
        if c == 0:
            squares[order] = square
            gates[order] = gate
            ups[order] = up
        else:
            squares[order] += square
            gates[order] += gate
            ups[order] += up

    def finish(order):
        start = (base, far)[order]
        each(1, half, lambda d: meta_copy(me, start + peer(d)).wait_recv())
        if order == 1:
            meta_copy(me, start + local).wait_recv()
        slot_weight = jnp.concatenate(
            [
                jnp.sum(diagonal * meta_recv[start + s][:1, :], axis=1, keepdims=True)
                for s in range(half)
            ],
            axis=0,
        )
        inverse = lax.rsqrt(squares[order] / width + 1e-6)
        gate = gates[order] * inverse
        weight = inverse * slot_weight
        hidden[order] = (gate / (1.0 + jnp.exp(-gate)) * (ups[order] * weight)).astype(BF16)
        block_rows = pl.ds(pl.multiple_of(start * cap, cap), half * cap)
        out = pltpu.make_async_copy(
            hidden.at[order], hidden_out.at[block_rows], local_sem.at[order]
        )
        out.start()
        return out

    heads_per_key = HQ // KVH
    def attend(c, scores):
        lanes = slice(c * WIDE, (c + 1) * WIDE)
        logs = jnp.concatenate(
            [logs_all[:, c * QUAD + i : c * QUAD + i + 1] for i in range(QUAD)], axis=0
        )
        row_max = jnp.maximum(jnp.max(scores, axis=1, keepdims=True), logs)
        powers = jnp.exp(scores - row_max).astype(BF16)
        carried = by_pair(
            jnp.broadcast_to(jnp.exp(logs - row_max), (QUAD * rows, WIDE // 2)),
            slice(0, WIDE // 2),
        )
        mixed = dot(powers, values[c * QUAD // heads_per_key])
        total = carried + by_pair(mixed, slice(WIDE // 2, WIDE))
        result = (
            carried * prior[:, lanes].astype(F32) + by_pair(mixed, slice(0, WIDE // 2))
        ) / total
        result = result.astype(BF16)
        raw[c] = result
        raw_copy(c).start()
        send[c] = dot(pick[...], result).astype(BF16)
        each(1, half, lambda d: row_copy(c, peer(d), send, row_send, me).start())
        out_copy(c).start()
        recv[c, slots_of(me), :] = send[c, slots_of(local), :]

    lag, near_lag, far_lag = 2, 3, 5
    ahead = scores_of(0)
    for c in range(chunks + far_lag):
        if c < chunks:
            scores = ahead
            if c + 1 < chunks:
                ahead = scores_of(c + 1)
            attend(c, scores)
        if c == 0:
            if_passing(ready)
        if c == 1:
            send_weights()
        if 0 <= c - lag < chunks:
            if_passing(functools.partial(pass_on, c - lag))
        if c == near_lag:
            loads[6].wait()
            loads[7].wait()
            loads[8].wait()
        if 0 <= c - near_lag < chunks:
            absorb(0, c - near_lag)
        if c - near_lag == chunks - 1:
            stores = [finish(0)]
        if 0 <= c - far_lag < chunks:
            absorb(1, c - far_lag)
    stores.append(finish(1))

    for one in passes:
        one.wait_send()
    rank_copy.wait_send()
    each(1, exp_total, lambda d: meta_copy(lax.rem(me + d, exp_total), me).wait_send())
    for c in range(chunks):
        raw_copy(c).wait_send()
        out_copy(c).wait()

    def sent(d):
        for c in range(chunks):
            row_copy(c, peer(d), send, row_send, me).wait_send()

    def passed_on():
        for c in range(chunks):
            for k in range(share):
                each(1, half, lambda d: relay_copy(c, k, peer(d)).wait_send())

    each(1, half, sent)
    if_passing(passed_on)
    for out in stores:
        out.wait()


def hand_over(attended, hidden, attended_out, hidden_out, rows_held, hidden_held, sems):
    fetches, stores = [], []
    pairs = ((attended, rows_held, attended_out), (hidden, hidden_held, hidden_out))
    for k, (source, held, target) in enumerate(pairs):
        step = source.shape[0] // PIECES
        for i in range(PIECES):
            part = pl.ds(i * step, step)
            fetches.append(pltpu.make_async_copy(source.at[part], held.at[part], sems.at[0, k, i]))
            stores.append(pltpu.make_async_copy(held.at[part], target.at[part], sems.at[1, k, i]))
    for fetch in fetches:
        fetch.start()
    for fetch, store in zip(fetches, stores):
        fetch.wait()
        store.start()
    for store in stores:
        store.wait()


def per_device(
    query, key_value, prior_out, prior_lse, norm_gain, w_gate, w_up, expert_ids, route_weight
):
    ctx_total = lax.axis_size("ctx")
    exp_total = lax.axis_size("exp")
    rows, width = query.shape[1:]
    hidden_width = w_gate.shape[2]
    capacity = max(2, IN_FLIGHT * rows * 3 // (2 * exp_total))
    cap = -(-capacity // 16) * 16
    chunks = width // WIDE
    pair_width = key_value.shape[2]
    any_space = pl.BlockSpec(memory_space=pl.ANY)
    dma = pltpu.SemaphoreType.DMA
    share = 2 if exp_total == 4 * CORES else 1
    slots = exp_total * cap
    half_slots = exp_total // 2 * cap
    attended, hidden = pl.pallas_call(
        functools.partial(kernel, ctx_total, exp_total, cap, share),
        out_shape=(
            jax.ShapeDtypeStruct((rows, width), BF16),
            jax.ShapeDtypeStruct((slots, hidden_width), BF16),
        ),
        in_specs=[any_space] * 9,
        out_specs=(any_space, any_space),
        scratch_shapes=[
            pltpu.VMEM((rows, width), BF16),
            pltpu.VMEM((rows, pair_width), BF16),
            pltpu.VMEM((rows, width), BF16),
            pltpu.VMEM((HQ, rows), F32),
            pltpu.VMEM((1, width), F32),
            pltpu.VMEM(w_gate.shape[1:], BF16),
            pltpu.VMEM(w_up.shape[1:], BF16),
            pltpu.VMEM((IN_FLIGHT, rows), jnp.int32),
            pltpu.VMEM((IN_FLIGHT, rows), BF16),
            pltpu.VMEM((STEPS - 1, rows, pair_width), BF16),
            pltpu.VMEM((KVH, STEPS * rows, WIDE), BF16),
            pltpu.VMEM((KVH, STEPS * rows, WIDE), BF16),
            pltpu.VMEM((chunks, rows, WIDE), BF16),
            pltpu.VMEM((half_slots, rows), BF16),
            pltpu.VMEM((share, half_slots, rows), BF16),
            pltpu.VMEM((chunks, half_slots, WIDE), BF16),
            pltpu.VMEM((chunks, share, rows, WIDE), BF16),
            pltpu.VMEM((chunks, share, half_slots, WIDE), BF16),
            pltpu.VMEM((chunks, slots, WIDE), BF16),
            pltpu.VMEM((exp_total, rows), F32),
            pltpu.VMEM((share, exp_total, rows), F32),
            pltpu.VMEM((exp_total, 8, rows), F32),
            pltpu.VMEM((exp_total, 8, rows), F32),
            pltpu.VMEM((2, half_slots, 1), F32),
            pltpu.VMEM((2, half_slots, hidden_width), F32),
            pltpu.VMEM((2, half_slots, hidden_width), F32),
            pltpu.VMEM((2, half_slots, hidden_width), BF16),
            dma((9,)),
            dma((chunks,)),
            dma((STEPS - 1,)),
            dma((STEPS - 1,)),
            dma((chunks, exp_total // 2)),
            dma((chunks, exp_total)),
            dma((chunks, share, exp_total // 2)),
            dma((chunks,)),
            dma((chunks, share)),
            dma((share + 1,)),
            dma((exp_total,)),
            dma((exp_total,)),
        ],
        compiler_params=pltpu.CompilerParams(
            collective_id=0, has_side_effects=True, vmem_limit_bytes=60 * 1024 * 1024
        ),
    )(
        query[0], key_value[0], prior_out[0], prior_lse[0].T, norm_gain[None], w_gate[0], w_up[0],
        expert_ids[0].T, route_weight[0].T,
    )
    attended, hidden = pl.pallas_call(
        hand_over,
        out_shape=(
            jax.ShapeDtypeStruct((rows, width), BF16),
            jax.ShapeDtypeStruct((slots, hidden_width), BF16),
        ),
        in_specs=[any_space] * 2,
        out_specs=(any_space, any_space),
        scratch_shapes=[
            pltpu.VMEM((rows, width), BF16),
            pltpu.VMEM((slots, hidden_width), BF16),
            dma((2, 2, PIECES)),
        ],
        compiler_params=pltpu.CompilerParams(vmem_limit_bytes=60 * 1024 * 1024),
    )(attended, hidden)
    hidden = hidden.reshape(exp_total, cap, hidden_width)[:, :capacity]
    return (attended[None], hidden.reshape(1, 1, exp_total * capacity, hidden_width))


def solution(mesh):
    placed = (
        P("exp", "ctx", None),
        P("exp", "ctx", None),
        P("exp", "ctx", None),
        P("exp", "ctx", None),
        P(),
        P("exp", None, None),
        P("exp", None, None),
        P("exp", "ctx", None),
        P("exp", "ctx", None),
    )
    return jax.shard_map(
        per_device,
        mesh=mesh,
        in_specs=placed,
        out_specs=(P("exp", "ctx", None), P("ctx", "exp", None, None)),
        check_vma=False,
    )
```

```python
import functools

import jax
import jax.numpy as jnp
from jax import lax
from jax.experimental import pallas as pl
from jax.experimental.pallas import tpu as pltpu
from jax.sharding import PartitionSpec as P

HQ = 32
KVH = 2
HD = 64
FF = 768
STEPS = 3
IN_FLIGHT = 2

MESH = pl.DeviceIdType.MESH
WIDE = 256
QUAD = WIDE // HD
PIECES = 4
CORES = 2
F32 = jnp.float32
BF16 = jnp.bfloat16


def dot(a, b, contract=((1,), (0,))):
    return lax.dot_general(a, b, (contract, ((), ())), preferred_element_type=F32)


def iota(shape, dim):
    return lax.broadcasted_iota(jnp.int32, shape, dim)


def positions(block, offset, rows, total):
    half = rows // 2
    return jnp.where(
        offset < half, block * half + offset, (2 * total - 1 - block) * half + offset - half
    )


def each(first, last, body):
    if last - first <= 8:
        for d in range(first, last):
            body(d)
    else:
        lax.fori_loop(first, last, lambda d, _: (body(d), 0)[1], 0)


def slot_rows(rank_ref, base, count, cap, rows):
    slot = iota((cap, rows), 0).astype(F32)
    return jnp.concatenate(
        [(slot == rank_ref[pl.ds(base + e, 1), :]).astype(BF16) for e in range(count)], axis=0
    )


def kernel(
    ctx_total, exp_total, cap, share,
    query, key_value, prior_out, prior_lse, gain, w_gate, w_up, ids, weights,
    attended_out, hidden_out,
    q, kv, prior, lse, scale, wg, wu, id_rows, weight_rows,
    window, keys, values, raw, pick, relay_pick, send, relay_in, relay_out, recv,
    rank_send, rank_recv, meta_send, meta_recv, squares, gates, ups, hidden,
    local_sem, out_sem, kv_send, kv_recv, row_send, row_recv, relay_send,
    raw_send, raw_recv, rank_sems, meta_send_sem, meta_recv_sem,
):
    rows = q.shape[0]
    width = q.shape[1]
    chunks = width // WIDE
    half = exp_total // 2
    me = lax.axis_index("exp")
    ctx = lax.axis_index("ctx")
    side = me // half
    base = side * half
    local = me - base
    far = half - base
    paired = share > 1
    core = lax.rem(me, CORES)
    if paired:
        across = half + core - CORES * side
        passes_on = me == half + core - CORES * (1 - side)
        place = local // CORES
        served = [far + core + CORES * k for k in range(share)]
    else:
        across = lax.rem(me + half, exp_total)
        passes_on = None
        place = 0
        served = [across]

    def if_passing(body):
        if paired:
            pl.when(passes_on)(body)
        else:
            body()


    loads = [
        pltpu.make_async_copy(a, b, local_sem.at[i])
        for i, (a, b) in enumerate(
            (
                (key_value, kv), (ids, id_rows), (weights, weight_rows), (prior_lse, lse),
                (query, q), (prior_out, prior), (gain, scale), (w_gate, wg), (w_up, wu),
            )
        )
    ]
    for load in loads:
        load.start()

    steps = sorted({d % ctx_total for j in range(1, STEPS) for d in (j, -j)})
    barrier = pltpu.get_barrier_semaphore()
    for d in steps:
        pl.semaphore_signal(
            barrier, inc=1, device_id={"ctx": lax.rem(ctx + d, ctx_total)}, device_id_type=MESH
        )

    def greet(d):
        pl.semaphore_signal(
            barrier, inc=1, device_id={"exp": lax.rem(me + d, exp_total)}, device_id_type=MESH
        )

    each(1, exp_total, greet)

    loads[1].wait()
    loads[2].wait()
    experts = iota((exp_total, rows), 0)
    named = jnp.zeros((exp_total, rows), F32)
    named_weight = jnp.zeros((exp_total, rows), F32)
    for j in range(IN_FLIGHT):
        hit = (experts == id_rows[j : j + 1, :]).astype(F32)
        named = named + hit
        named_weight = named_weight + hit * weight_rows[j : j + 1, :].astype(F32)
    earlier = (iota((rows, rows), 0) < iota((rows, rows), 1)).astype(BF16)
    rank_send[...] = jnp.where(named > 0.5, dot(named.astype(BF16), earlier), -1.0)
    loads[0].wait()
    pl.semaphore_wait(barrier, exp_total - 1 + len(steps))

    passes = [
        pltpu.make_async_remote_copy(
            src_ref=kv, dst_ref=window.at[j - 1],
            send_sem=kv_send.at[j - 1], recv_sem=kv_recv.at[j - 1],
            device_id={"ctx": lax.rem(ctx + j, ctx_total)}, device_id_type=MESH,
        )
        for j in range(1, STEPS)
    ]
    for one in passes:
        one.start()
    rank_copy = pltpu.make_async_remote_copy(
        src_ref=rank_send, dst_ref=rank_recv.at[place], send_sem=rank_sems.at[share],
        recv_sem=rank_sems.at[place], device_id={"exp": across}, device_id_type=MESH,
    )
    rank_copy.start()
    pick[...] = slot_rows(rank_send, base, half, cap, rows)

    own = iota((rows, 1), 0)
    query_pos = positions(ctx, own, rows, ctx_total)
    bias = []
    for j in range(STEPS):
        source = lax.rem(ctx - j + ctx_total, ctx_total)
        key_pos = positions(source, iota((1, rows), 1), rows, ctx_total)
        bias.append(jnp.where(key_pos <= query_pos, 0.0, -1e30))
    bias = jnp.concatenate(bias, axis=1)
    bias = jnp.concatenate([bias] * QUAD, axis=0)

    place_row = iota((KVH * HD, WIDE), 0)
    place_lane = iota((KVH * HD, WIDE), 1)
    lane_head = iota((rows, WIDE), 1) // HD
    lane = iota((rows, WIDE // 2), 1)

    def lay_out(j):
        block = kv[...] if j == 0 else window[j - 1]
        block_keys = block[:, : KVH * HD] * jnp.asarray(HD ** (-0.5), BF16)
        block_values = block[:, KVH * HD :]
        at = slice(j * rows, (j + 1) * rows)
        for g in range(KVH):
            place = (place_row == lax.rem(place_lane, HD) + g * HD).astype(BF16)
            keys[g, at, :] = dot(block_keys, place).astype(BF16)
            tiled = dot(block_values, place)
            values[g, at, :] = jnp.where(lane_head < QUAD // 2, tiled, 1.0).astype(BF16)

    lay_out(0)
    loads[3].wait()
    logs_all = jnp.transpose(lse[...])
    loads[4].wait()
    loads[5].wait()
    for j in range(1, STEPS):
        passes[j - 1].wait_recv()
        lay_out(j)

    def slots_of(index):
        return pl.ds(pl.multiple_of(index * cap, cap), cap)

    def row_copy(c, to_local, source_ref, sems, source):
        return pltpu.make_async_remote_copy(
            src_ref=source_ref.at[c, slots_of(to_local)],
            dst_ref=recv.at[c, slots_of(source)],
            send_sem=sems.at[c, to_local], recv_sem=row_recv.at[c, source],
            device_id={"exp": base + to_local}, device_id_type=MESH,
        )

    def peer(d):
        return lax.rem(local + d, half)

    def raw_copy(c):
        return pltpu.make_async_remote_copy(
            src_ref=raw.at[c], dst_ref=relay_in.at[c, place], send_sem=raw_send.at[c],
            recv_sem=raw_recv.at[c, place], device_id={"exp": across}, device_id_type=MESH,
        )

    def out_copy(c):
        return pltpu.make_async_copy(
            raw.at[c], attended_out.at[:, c * WIDE : (c + 1) * WIDE], out_sem.at[c]
        )

    def meta_copy(to, at):
        return pltpu.make_async_remote_copy(
            src_ref=meta_send.at[to], dst_ref=meta_recv.at[at],
            send_sem=meta_send_sem.at[to], recv_sem=meta_recv_sem.at[at],
            device_id={"exp": to}, device_id_type=MESH,
        )

    def relay_copy(c, k, to_local):
        return pltpu.make_async_remote_copy(
            src_ref=relay_out.at[c, k, slots_of(to_local)],
            dst_ref=recv.at[c, slots_of(served[k])],
            send_sem=relay_send.at[c, k, to_local], recv_sem=row_recv.at[c, served[k]],
            device_id={"exp": base + to_local}, device_id_type=MESH,
        )

    def pass_on(c):
        for k in range(share):
            pltpu.make_async_remote_copy(
                src_ref=raw.at[c], dst_ref=relay_in.at[c, k], send_sem=raw_send.at[c],
                recv_sem=raw_recv.at[c, k], device_id={"exp": across}, device_id_type=MESH,
            ).wait_recv()
            relay_out[c, k] = dot(relay_pick[k], relay_in[c, k]).astype(BF16)
            each(1, half, lambda d, k=k: relay_copy(c, k, peer(d)).start())
            recv[c, slots_of(served[k]), :] = relay_out[c, k, slots_of(local), :]

    def ready():
        for k in range(share):
            pltpu.make_async_remote_copy(
                src_ref=rank_send, dst_ref=rank_recv.at[k], send_sem=rank_sems.at[share],
                recv_sem=rank_sems.at[k], device_id={"exp": across}, device_id_type=MESH,
            ).wait_recv()
            relay_pick[k] = slot_rows(rank_recv.at[k], base, half, cap, rows)

    diagonal = (iota((cap, rows), 0) == iota((cap, rows), 1)).astype(F32)

    def send_weights():
        slot = iota((cap, rows), 0).astype(F32)
        for e in range(exp_total):
            chosen = slot == rank_send[e : e + 1, :]
            column = jnp.sum(
                jnp.where(chosen, named_weight[e : e + 1, :], 0.0), axis=1, keepdims=True
            )
            line = jnp.sum(diagonal * column, axis=0, keepdims=True)
            meta_send[e] = jnp.broadcast_to(line, (8, rows))
        each(1, exp_total, lambda d: meta_copy(lax.rem(me + d, exp_total), me).start())
        meta_recv[me] = meta_send[me]

    def scores_of(c):
        g = c * QUAD // heads_per_key
        four = q[:, c * WIDE : (c + 1) * WIDE]
        none = jnp.zeros((), BF16)
        stacked = jnp.concatenate(
            [jnp.where(lane_head == i, four, none) for i in range(QUAD)], axis=0
        )
        return dot(stacked, keys[g], ((1,), (1,))) + bias

    def by_pair(parts, lanes):
        return jnp.concatenate(
            [
                jnp.where(
                    lane < HD,
                    parts[p * rows : (p + 1) * rows, lanes],
                    parts[(p + 1) * rows : (p + 2) * rows, lanes],
                )
                for p in range(0, QUAD, 2)
            ],
            axis=1,
        )

    def await_rows(order, c):
        if order == 1 and paired:
            for k in range(share):
                row_copy(c, local, send, row_send, far + 1 - core + CORES * k).wait_recv()

            @pl.when(jnp.logical_not(passes_on))
            def _():
                for k in range(share):
                    row_copy(c, local, send, row_send, served[k]).wait_recv()
        else:
            start = (base, far)[order]
            each(
                1, half,
                lambda d: row_copy(c, local, send, row_send, start + peer(d)).wait_recv(),
            )

    def absorb(order, pair):
        start = (base, far)[order]
        block_rows = pl.ds(pl.multiple_of(start * cap, cap), half * cap)
        for c in (2 * pair, 2 * pair + 1):
            await_rows(order, c)
        block = jnp.concatenate(
            [recv[c, block_rows, :].astype(F32) for c in (2 * pair, 2 * pair + 1)], axis=1
        )
        square = jnp.sum(block * block, axis=1, keepdims=True)
        lanes = slice(2 * pair * WIDE, (2 * pair + 2) * WIDE)
        scaled = (block * scale[:, lanes]).astype(BF16)
        gate = dot(scaled, wg[lanes, :])
        up = dot(scaled, wu[lanes, :])
        if pair == 0:
            squares[order] = square
            gates[order] = gate
            ups[order] = up
        else:
            squares[order] += square
            gates[order] += gate
            ups[order] += up

    def finish(order):
        start = (base, far)[order]
        each(1, half, lambda d: meta_copy(me, start + peer(d)).wait_recv())
        if order == 1:
            meta_copy(me, start + local).wait_recv()
        slot_weight = jnp.concatenate(
            [
                jnp.sum(diagonal * meta_recv[start + s][:1, :], axis=1, keepdims=True)
                for s in range(half)
            ],
            axis=0,
        )
        inverse = lax.rsqrt(squares[order] / width + 1e-6)
        gate = gates[order] * inverse
        weight = inverse * slot_weight
        hidden[order] = (gate / (1.0 + jnp.exp(-gate)) * (ups[order] * weight)).astype(BF16)
        block_rows = pl.ds(pl.multiple_of(start * cap, cap), half * cap)
        out = pltpu.make_async_copy(
            hidden.at[order], hidden_out.at[block_rows], local_sem.at[order]
        )
        out.start()
        return out

    heads_per_key = HQ // KVH
    def attend(c, scores):
        lanes = slice(c * WIDE, (c + 1) * WIDE)
        logs = jnp.concatenate(
            [logs_all[:, c * QUAD + i : c * QUAD + i + 1] for i in range(QUAD)], axis=0
        )
        row_max = jnp.maximum(jnp.max(scores, axis=1, keepdims=True), logs)
        powers = jnp.exp(scores - row_max).astype(BF16)
        carried = by_pair(
            jnp.broadcast_to(jnp.exp(logs - row_max), (QUAD * rows, WIDE // 2)),
            slice(0, WIDE // 2),
        )
        mixed = dot(powers, values[c * QUAD // heads_per_key])
        total = carried + by_pair(mixed, slice(WIDE // 2, WIDE))
        result = (
            carried * prior[:, lanes].astype(F32) + by_pair(mixed, slice(0, WIDE // 2))
        ) / total
        result = result.astype(BF16)
        raw[c] = result
        raw_copy(c).start()
        send[c] = dot(pick[...], result).astype(BF16)
        each(1, half, lambda d: row_copy(c, peer(d), send, row_send, me).start())
        out_copy(c).start()
        recv[c, slots_of(me), :] = send[c, slots_of(local), :]

    lag, near_lag, far_lag = 2, 5, 8
    ahead = scores_of(0)
    for c in range(chunks + far_lag):
        if c < chunks:
            scores = ahead
            if c + 1 < chunks:
                ahead = scores_of(c + 1)
            attend(c, scores)
        if c == 0:
            if_passing(ready)
        if c == 1:
            send_weights()
        if 0 <= c - lag < chunks:
            if_passing(functools.partial(pass_on, c - lag))
        if c == near_lag:
            loads[6].wait()
            loads[7].wait()
            loads[8].wait()
        if 0 <= c - near_lag < chunks and (c - near_lag) % 2 == 0:
            absorb(0, (c - near_lag) // 2)
        if c - near_lag == chunks - 1:
            stores = [finish(0)]
        if 0 <= c - far_lag < chunks and (c - far_lag) % 2 == 0:
            absorb(1, (c - far_lag) // 2)
    stores.append(finish(1))

    for one in passes:
        one.wait_send()
    rank_copy.wait_send()
    each(1, exp_total, lambda d: meta_copy(lax.rem(me + d, exp_total), me).wait_send())
    for c in range(chunks):
        raw_copy(c).wait_send()
        out_copy(c).wait()

    def sent(d):
        for c in range(chunks):
            row_copy(c, peer(d), send, row_send, me).wait_send()

    def passed_on():
        for c in range(chunks):
            for k in range(share):
                each(1, half, lambda d: relay_copy(c, k, peer(d)).wait_send())

    each(1, half, sent)
    if_passing(passed_on)
    for out in stores:
        out.wait()


def hand_over(attended, hidden, attended_out, hidden_out, rows_held, hidden_held, sems):
    fetches, stores = [], []
    pairs = ((attended, rows_held, attended_out), (hidden, hidden_held, hidden_out))
    for k, (source, held, target) in enumerate(pairs):
        step = source.shape[0] // PIECES
        for i in range(PIECES):
            part = pl.ds(i * step, step)
            fetches.append(pltpu.make_async_copy(source.at[part], held.at[part], sems.at[0, k, i]))
            stores.append(pltpu.make_async_copy(held.at[part], target.at[part], sems.at[1, k, i]))
    for fetch in fetches:
        fetch.start()
    for fetch, store in zip(fetches, stores):
        fetch.wait()
        store.start()
    for store in stores:
        store.wait()


def per_device(
    query, key_value, prior_out, prior_lse, norm_gain, w_gate, w_up, expert_ids, route_weight
):
    ctx_total = lax.axis_size("ctx")
    exp_total = lax.axis_size("exp")
    rows, width = query.shape[1:]
    hidden_width = w_gate.shape[2]
    capacity = max(2, IN_FLIGHT * rows * 3 // (2 * exp_total))
    cap = -(-capacity // 16) * 16
    chunks = width // WIDE
    pair_width = key_value.shape[2]
    any_space = pl.BlockSpec(memory_space=pl.ANY)
    dma = pltpu.SemaphoreType.DMA
    share = 2 if exp_total == 4 * CORES else 1
    slots = exp_total * cap
    half_slots = exp_total // 2 * cap
    attended, hidden = pl.pallas_call(
        functools.partial(kernel, ctx_total, exp_total, cap, share),
        out_shape=(
            jax.ShapeDtypeStruct((rows, width), BF16),
            jax.ShapeDtypeStruct((slots, hidden_width), BF16),
        ),
        in_specs=[any_space] * 9,
        out_specs=(any_space, any_space),
        scratch_shapes=[
            pltpu.VMEM((rows, width), BF16),
            pltpu.VMEM((rows, pair_width), BF16),
            pltpu.VMEM((rows, width), BF16),
            pltpu.VMEM((HQ, rows), F32),
            pltpu.VMEM((1, width), F32),
            pltpu.VMEM(w_gate.shape[1:], BF16),
            pltpu.VMEM(w_up.shape[1:], BF16),
            pltpu.VMEM((IN_FLIGHT, rows), jnp.int32),
            pltpu.VMEM((IN_FLIGHT, rows), BF16),
            pltpu.VMEM((STEPS - 1, rows, pair_width), BF16),
            pltpu.VMEM((KVH, STEPS * rows, WIDE), BF16),
            pltpu.VMEM((KVH, STEPS * rows, WIDE), BF16),
            pltpu.VMEM((chunks, rows, WIDE), BF16),
            pltpu.VMEM((half_slots, rows), BF16),
            pltpu.VMEM((share, half_slots, rows), BF16),
            pltpu.VMEM((chunks, half_slots, WIDE), BF16),
            pltpu.VMEM((chunks, share, rows, WIDE), BF16),
            pltpu.VMEM((chunks, share, half_slots, WIDE), BF16),
            pltpu.VMEM((chunks, slots, WIDE), BF16),
            pltpu.VMEM((exp_total, rows), F32),
            pltpu.VMEM((share, exp_total, rows), F32),
            pltpu.VMEM((exp_total, 8, rows), F32),
            pltpu.VMEM((exp_total, 8, rows), F32),
            pltpu.VMEM((2, half_slots, 1), F32),
            pltpu.VMEM((2, half_slots, hidden_width), F32),
            pltpu.VMEM((2, half_slots, hidden_width), F32),
            pltpu.VMEM((2, half_slots, hidden_width), BF16),
            dma((9,)),
            dma((chunks,)),
            dma((STEPS - 1,)),
            dma((STEPS - 1,)),
            dma((chunks, exp_total // 2)),
            dma((chunks, exp_total)),
            dma((chunks, share, exp_total // 2)),
            dma((chunks,)),
            dma((chunks, share)),
            dma((share + 1,)),
            dma((exp_total,)),
            dma((exp_total,)),
        ],
        compiler_params=pltpu.CompilerParams(
            collective_id=0, has_side_effects=True, vmem_limit_bytes=60 * 1024 * 1024
        ),
    )(
        query[0], key_value[0], prior_out[0], prior_lse[0].T, norm_gain[None], w_gate[0], w_up[0],
        expert_ids[0].T, route_weight[0].T,
    )
    attended, hidden = pl.pallas_call(
        hand_over,
        out_shape=(
            jax.ShapeDtypeStruct((rows, width), BF16),
            jax.ShapeDtypeStruct((slots, hidden_width), BF16),
        ),
        in_specs=[any_space] * 2,
        out_specs=(any_space, any_space),
        scratch_shapes=[
            pltpu.VMEM((rows, width), BF16),
            pltpu.VMEM((slots, hidden_width), BF16),
            dma((2, 2, PIECES)),
        ],
        compiler_params=pltpu.CompilerParams(vmem_limit_bytes=60 * 1024 * 1024),
    )(attended, hidden)
    hidden = hidden.reshape(exp_total, cap, hidden_width)[:, :capacity]
    return (attended[None], hidden.reshape(1, 1, exp_total * capacity, hidden_width))


def solution(mesh):
    placed = (
        P("exp", "ctx", None),
        P("exp", "ctx", None),
        P("exp", "ctx", None),
        P("exp", "ctx", None),
        P(),
        P("exp", None, None),
        P("exp", None, None),
        P("exp", "ctx", None),
        P("exp", "ctx", None),
    )
    return jax.shard_map(
        per_device,
        mesh=mesh,
        in_specs=placed,
        out_specs=(P("exp", "ctx", None), P("ctx", "exp", None, None)),
        check_vma=False,
    )
```
